128 devices in a mesh: slab: 16 (over z, y), sub: 8 (over x, core).
Axes of the slice: x: 4, y: 4, z: 4, core: 2. Of those that a mesh axis runs over, the one named last changes fastest.
Arguments:
- multipole: bfloat16 [456, 65536], P(None, ('slab', 'sub')), may hold values from -6 to 6
- send_list: int32 [128, 8, 128], P(('slab', 'sub')), may hold values from -1 to 511, as said below
- source_slot: int32 [64, 65536], P(None, ('slab', 'sub')), may hold values from -1 to 1535, as said below
- m2l_ops: bfloat16 [64, 456, 456], P('slab'), may hold values from -0.03125 to 0.03125
- l2l_ops: bfloat16 [8, 456, 456], replicated, may hold values from -0.25 to 0.25
- coarse_exp: bfloat16 [456, 128], P(None, 'sub'), may hold values from -6 to 6
Outputs:
- local_exp: bfloat16 [456, 65536], P(None, ('slab', 'sub'))
The draws below stay inside these ranges and needn't reach their ends.
Inputs may be any that keep to these rules, and one draw needn't show every extreme that they name: send_list[o, n] holds, in its first slots, between 1 and 128 distinct positions of boxes on device o where the device in direction n exists, and -1 in all slots where it does not; in every draw some device fills all 128 slots toward each of its neighbours. source_slot[k, t] is -1 (no interaction), a position below 512 of a box on the target's own device, or 512 + n * 128 + j for a filled slot j of send_list[o, n] with o the target device's neighbour in the direction opposite to n.
All inputs are finite; a program needn't handle non-finite values.
Results may differ from the reference program's by a relative error of at most 0.0051.
Values may be sent and summed in bfloat16 or wider, within the bound.
A program may use at most 128 MiB of HBM per device.

```python
import jax
import jax.numpy as jnp
from jax import lax

COEF = 456
BOX_DEV = 512
OFFSETS = 64
CAP = 128
COLS = 1536
SENDERS = 128
BOXES = 65536
COARSE = 128
N_SLAB = 16
N_SUB = 8


DIR_SLAB = (-1, -1, -1, 0, 0, 1, 1, 1)


DIR_SUB = (-1, 0, 1, -1, 1, -1, 0, 1)


def ghost_counts(key):
    key = jax.random.fold_in(key, 11)
    key_count, key_row, key_col = jax.random.split(key, 3)
    counts = jax.random.randint(key_count, (SENDERS, 8), 1, CAP + 1)
    devices_line = jnp.arange(SENDERS, dtype=jnp.int32)
    rows_line = devices_line // N_SUB
    cols_line = devices_line % N_SUB
    slab_steps = jnp.array(DIR_SLAB, dtype=jnp.int32)
    sub_steps = jnp.array(DIR_SUB, dtype=jnp.int32)
    dest_row = rows_line[:, None] + slab_steps[None, :]
    dest_col = cols_line[:, None] + sub_steps[None, :]
    exists = (dest_row >= 0) & (dest_row < N_SLAB) & (dest_col >= 0) & (dest_col < N_SUB)
    full_row = jax.random.randint(key_row, (), 0, N_SLAB - 1)
    full_col = jax.random.randint(key_col, (), 0, N_SUB - 1)
    full_sender = full_row * N_SUB + full_col
    counts = jnp.where(devices_line[:, None] == full_sender, CAP, counts)
    return jnp.where(exists, counts, 0)


def draw_send_list(key, part):
    counts = ghost_counts(key)
    key = jax.random.fold_in(key, 1)
    scores = jax.random.randint(key, (SENDERS, 8, BOX_DEV), 0, 1 << 18) * BOX_DEV + jnp.arange(BOX_DEV, dtype=jnp.int32)
    order = jnp.argsort(scores, axis=-1)[..., :CAP]
    filled = jnp.arange(CAP, dtype=jnp.int32)[None, None, :] < counts[:, :, None]
    return jnp.where(filled, order, -1).astype(jnp.int32)


def draw_source_slot(key, part):
    counts = ghost_counts(key)
    key = jax.random.fold_in(key, 2)
    key_region, key_slot, key_own, key_live = jax.random.split(key, 4)
    targets = jnp.arange(BOXES, dtype=jnp.int32)[None, :]
    device_id = targets // BOX_DEV
    target_row = device_id // N_SUB
    target_col = device_id % N_SUB
    slab_steps = jnp.array(DIR_SLAB, dtype=jnp.int32)
    sub_steps = jnp.array(DIR_SUB, dtype=jnp.int32)
    region = jax.random.randint(key_region, (OFFSETS, BOXES), 0, 9)
    direction = jnp.clip(region - 1, 0, 7)
    owner_row = target_row - slab_steps[direction]
    owner_col = target_col - sub_steps[direction]
    exists = (owner_row >= 0) & (owner_row < N_SLAB) & (owner_col >= 0) & (owner_col < N_SUB)
    owner_id = jnp.clip(owner_row, 0, N_SLAB - 1) * N_SUB + jnp.clip(owner_col, 0, N_SUB - 1)
    have = jnp.where(exists, counts[owner_id, direction], 0)
    slot_pick = jax.random.randint(key_slot, (OFFSETS, BOXES), 0, jnp.maximum(have, 1))
    own_pick = jax.random.randint(key_own, (OFFSETS, BOXES), 0, BOX_DEV)
    use_ghost = (region > 0) & (have > 0)
    value = jnp.where(use_ghost, BOX_DEV + direction * CAP + slot_pick, own_pick)
    live = jax.random.randint(key_live, (OFFSETS, BOXES), 0, 4) > 0
    return jnp.where(live, value, -1).astype(jnp.int32)


def block_levels(stream_key, shape, shards, low, high):
    level, own = 1.0, jax.random.fold_in(stream_key, 6)
    for position, shards_of in shards:
        draws = jnp.exp(jax.random.uniform(jax.random.fold_in(own, position), (shards_of,), jnp.float32, low / len(shards), high / len(shards)))
        level = level * jnp.repeat(draws, shape[position] // shards_of).reshape([-1 if axis == position else 1 for axis in range(len(shape))])
    return level


def centred(stream_key, extent, deviation, reach, shards=(), kind=jnp.bfloat16):
    factor_of = block_levels(stream_key, extent, shards, -0.22, 0.18) if shards else 1.0
    entries = jax.random.normal(stream_key, extent, jnp.float32) * deviation * factor_of
    return jnp.minimum(jnp.maximum(entries, -reach), reach).astype(kind)


def setup_inputs(seed: int = 0) -> dict:
    splits = jax.random.split(jax.random.key(seed), 7)
    return {
        "multipole": centred(splits[0], (COEF, BOXES), 1.0, 6.0, ((1, 128),)),
        "send_list": draw_send_list(jax.random.fold_in(splits[6], 71), 0),
        "source_slot": draw_source_slot(jax.random.fold_in(splits[6], 71), 0),
        "m2l_ops": centred(splits[3], (OFFSETS, COEF, COEF), (COEF * OFFSETS) ** -0.5, 0.03125, ((0, 16),)),
        "l2l_ops": centred(splits[4], (8, COEF, COEF), COEF ** -0.5, 0.25),
        "coarse_exp": centred(splits[5], (COEF, COARSE), 1.0, 6.0, ((1, 8),)),
    }


DIR_SLAB = (-1, -1, -1, 0, 0, 1, 1, 1)
DIR_SUB = (-1, 0, 1, -1, 1, -1, 0, 1)


def descend(operators, parents):
    children = jnp.einsum("ock,kp->cpo", operators.astype(jnp.float32), parents.astype(jnp.float32))
    return children.reshape(parents.shape[0], -1)


def reference(multipole, send_list, source_slot, m2l_ops, l2l_ops, coarse_exp):
    targets = jnp.arange(BOXES, dtype=jnp.int32)
    device_id = targets // BOX_DEV
    target_row = device_id // N_SUB
    target_col = device_id % N_SUB
    slab_steps = jnp.array(DIR_SLAB, dtype=jnp.int32)
    sub_steps = jnp.array(DIR_SUB, dtype=jnp.int32)
    present = source_slot >= 0
    clipped = jnp.clip(source_slot, 0, COLS - 1)
    is_ghost = clipped >= BOX_DEV
    ghost_place = jnp.clip(clipped - BOX_DEV, 0, 8 * CAP - 1)
    direction = ghost_place // CAP
    slot_index = ghost_place % CAP
    owner_row = jnp.clip(target_row[None, :] - slab_steps[direction], 0, N_SLAB - 1)
    owner_col = jnp.clip(target_col[None, :] - sub_steps[direction], 0, N_SUB - 1)
    owner_id = (owner_row * N_SUB + owner_col).astype(jnp.int32)
    sent_box = jnp.clip(send_list[owner_id, direction, slot_index], 0, BOX_DEV - 1)
    own_box = device_id[None, :] * BOX_DEV + jnp.clip(clipped, 0, BOX_DEV - 1)
    global_box = jnp.where(is_ghost, owner_id * BOX_DEV + sent_box, own_box).astype(jnp.int32)

    def one_offset(running, operand_pair):
        weight, column_ids, present_mask = operand_pair
        columns = jnp.take(multipole, column_ids, axis=1)
        columns = jnp.where(present_mask[None, :], columns, jnp.zeros((), multipole.dtype))
        return running + jnp.dot(weight, columns, preferred_element_type=jnp.float32), None

    summed, _ = lax.scan(one_offset, jnp.zeros((COEF, BOXES), jnp.float32), (m2l_ops, global_box, present))
    level_one = descend(l2l_ops, coarse_exp).astype(jnp.bfloat16)
    level_two = descend(l2l_ops, level_one).astype(jnp.bfloat16)
    finest = descend(l2l_ops, level_two)
    return (summed + finest).astype(jnp.bfloat16)
```

```python
import jax
import jax.numpy as jnp
from jax import lax
from jax.experimental import pallas as pl
from jax.experimental.pallas import tpu as pltpu
from jax.sharding import PartitionSpec as P

DIR_SLAB = (-1, -1, -1, 0, 0, 1, 1, 1)
DIR_SUB = (-1, 0, 1, -1, 1, -1, 0, 1)
COEF, BOX, OFFSETS, CAP, COLS = 456, 512, 64, 128, 1536
LANES = 512
NT = (((1,), (1,)), ((), ()))
MESH = pl.DeviceIdType.MESH
AHEAD = 3
LATE = 1


def pick_rows(index_of, table_ref, picked_ref, unroll):
    def chunk(i, carry):
        for u in range(64):
            place = pl.multiple_of(i * 256 + (u // 8) * 32, 32) + u % 8
            picked_ref[pl.ds(place, 4, stride=8), :] = table_ref[index_of(i * 64 + u)]
        return carry
    lax.fori_loop(0, BOX // 64, chunk, 0, unroll=unroll)


def spread_rows(picked_ref, table_ref, first):
    def chunk(i, carry):
        for u in range(64):
            place = pl.multiple_of(i * 256 + (u // 8) * 32, 32) + u % 8
            table_ref[first + i * 64 + u] = picked_ref[pl.ds(place, 4, stride=8), :]
        return carry
    lax.fori_loop(0, BOX // 64, chunk, 0)


def picked_value(picked_ref):
    tiles = picked_ref[...].reshape(BOX // 8, 4, 8, 128)
    return jnp.concatenate(
        [tiles[:, c].reshape(BOX, 128) for c in range(4)], axis=1
    ).astype(jnp.bfloat16)


def set_picked(picked_ref, rows):
    tiles = [rows[:, c * 128 : (c + 1) * 128].reshape(BOX // 8, 8, 128) for c in range(4)]
    picked_ref[...] = jnp.stack(tiles, axis=1).reshape(BOX * 4, 128)


def pad_lanes(rows):
    return jnp.concatenate([rows, jnp.zeros((rows.shape[0], LANES - COEF), rows.dtype)], axis=1)


def kernel(
    multipole_ref, send_list_ref, slot_hbm, ops_hbm, l2l_hbm, coarse_ref, out_ref,
    slot_ref, ops_ref, l2l_ref, table_ref, even_ref, odd_ref, acc_ref, ghost_out, ghost_in,
    coarse_out, coarse_in, level_one, level_two,
    local_sem, op_send, op_recv, ghost_send, ghost_recv, coarse_send, coarse_recv,
):
    a, b = lax.axis_index("slab"), lax.axis_index("sub")
    z, y, x, core = a // 4, a % 4, b // 2, b % 2

    local = [
        pltpu.make_async_copy(slot_hbm, slot_ref, local_sem.at[0]),
        pltpu.make_async_copy(l2l_hbm, l2l_ref, local_sem.at[1]),
        pltpu.make_async_copy(ops_hbm, ops_ref.at[pl.ds(4 * a, 4)], local_sem.at[2]),
    ]
    for copy in local:
        copy.start()

    def exists(da, db):
        row, col = a + da, b + db
        return (row >= 0) & (row < 16) & (col >= 0) & (col < 8)

    ghost_in[...] = jnp.zeros_like(ghost_in)
    barrier = pltpu.get_barrier_semaphore()
    for step in range(1, 8):
        pl.semaphore_signal(barrier, inc=1, device_id=(a, (b + step) % 8), device_id_type=MESH)
    for dy, dz in ((1, 0), (3, 0), (0, 1), (0, 3)):
        there = ((z + dz) % 4) * 4 + (y + dy) % 4
        pl.semaphore_signal(barrier, inc=1, device_id=(there, b), device_id_type=MESH)
    greeted = 11
    for da, db in zip(DIR_SLAB, DIR_SUB):
        if da != 0:
            here = exists(da, db)

            @pl.when(here)
            def _():
                pl.semaphore_signal(barrier, inc=1, device_id=(a + da, b + db), device_id_type=MESH)

            greeted = greeted + here.astype(jnp.int32)

    own = jnp.concatenate(
        [multipole_ref[...].astype(jnp.float32), jnp.zeros((LANES - COEF, BOX), jnp.float32)], axis=0
    ).T
    set_picked(even_ref, own)
    table_ref[0] = jnp.zeros((4, 128), jnp.float32)
    spread_rows(even_ref, table_ref, 1)
    coarse = jnp.concatenate(
        [coarse_ref[...].astype(jnp.float32), jnp.zeros((LANES - COEF, 128), jnp.float32)], axis=0
    ).T
    coarse_out[...] = coarse[:16]

    pl.semaphore_wait(barrier, greeted)

    def source(cls, carrier, q1, q2):
        sign = 1 - 2 * carrier
        first = (q1 + (q1 == 2).astype(jnp.int32) - (q1 == 3).astype(jnp.int32)) * sign
        second = (q2 + (q2 == 2).astype(jnp.int32) - (q2 == 3).astype(jnp.int32)) * sign
        y0 = (y - jnp.where(cls == 0, first, second) + 4) % 4
        z0 = (z - jnp.where(cls == 0, second, first) + 4) % 4
        return y0, z0, 4 * (4 * z0 + y0) + 2 * carrier + cls

    sign = 1 - 2 * core

    def links(cls, q1, q2, own_op):
        y0, z0, k = source(cls, core, q1, q2)
        half = (x + y0 + z0 + cls) % 2 == 0
        number = k // 4 * 2 + cls
        src = ops_hbm.at[2 * core + cls] if own_op else ops_ref.at[k]

        def copy(kind, device):
            return pltpu.make_async_remote_copy(
                src_ref=src, dst_ref=ops_ref.at[k], send_sem=op_send.at[kind, number],
                recv_sem=op_recv.at[k], device_id=device, device_id_type=MESH,
            )

        def along(axis_is_y, by):
            ny = jnp.where(axis_is_y, (y + by + 4) % 4, y)
            nz = jnp.where(axis_is_y, z, (z + by + 4) % 4)
            return (4 * nz + ny, b)

        prim_y = cls == 0
        back = along(~prim_y, -sign)
        beside = (a, ((x + sign + 4) % 4) * 2 + core)
        kinds = [
            ((q2 == 0) & (q1 <= 1), lambda: copy(0, along(prim_y, sign))),
            ((q2 == 0) & (q1 == 0), lambda: copy(1, along(prim_y, -sign))),
            ((q2 == 0) | ((q2 == 1) & half), lambda: copy(2, along(~prim_y, sign))),
            (
                ((q2 == 0) | (q2 >= 2)) & half,
                lambda: copy(3, (jnp.where(q2 == 0, back[0], a), jnp.where(q2 == 0, b, beside[1]))),
            ),
            (q1 + q2 > 0, lambda: copy(4, (a, b + sign))),
        ]
        return k, kinds

    zero = jnp.int32(0)

    def start_own(cls, kinds):
        _, found = links(jnp.int32(cls), zero, zero, True)
        for kind in kinds:
            @pl.when(found[kind][0])
            def _():
                found[kind][1]().start()

    def over_x(cls, step):
        y0, z0, _ = source(cls, core, step % 4, step // 4)
        return (step >= 8) & ((x + y0 + z0 + cls) % 2 == 1)

    def forward(cls, step):
        k, found = links(cls, step % 4, step // 4, False)
        pltpu.make_async_copy(ops_ref.at[k], ops_ref.at[k], op_recv.at[k]).wait()
        for condition, copy in found:
            @pl.when(condition)
            def _():
                copy().start()

    start_own(0, (0, 1))
    start_own(1, (0, 1))

    has_coarse = b == a // 2

    def coarse_copy(step):
        return pltpu.make_async_remote_copy(
            src_ref=coarse_out.at[pl.ds(pl.multiple_of(a % 2 * 8, 8), 8)], dst_ref=coarse_in,
            send_sem=coarse_send.at[step - 1], recv_sem=coarse_recv,
            device_id=(a, (b + step) % 8), device_id_type=MESH,
        )

    @pl.when(has_coarse)
    def _():
        for step in range(1, 8):
            coarse_copy(step).start()
        coarse_in[...] = coarse_out[pl.ds(pl.multiple_of(a % 2 * 8, 8), 8), :]

    def ghost_copy(n):
        da, db = DIR_SLAB[n], DIR_SUB[n]
        return pltpu.make_async_remote_copy(
            src_ref=ghost_out.at[n], dst_ref=ghost_in.at[n], send_sem=ghost_send.at[n],
            recv_sem=ghost_recv.at[n], device_id=(a + da, b + db), device_id_type=MESH,
        )

    for part in range(2):
        pick_rows(
            lambda t: jnp.maximum(send_list_ref[0, 4 * part + t // CAP, t % CAP], 0) + 1,
            table_ref, odd_ref, False,
        )
        ghost_out[4 * part : 4 * part + 4] = picked_value(odd_ref).reshape(4, CAP, LANES)
        for n in range(4 * part, 4 * part + 4):
            @pl.when(exists(DIR_SLAB[n], DIR_SUB[n]))
            def _():
                ghost_copy(n).start()

    start_own(0, (2, 3))
    start_own(1, (2, 3))

    @pl.when(jnp.logical_not(has_coarse))
    def _():
        coarse_copy(1).wait_recv()
    local[1].wait()

    parent = jnp.broadcast_to(coarse_in[pl.ds(b, 1), :], (8, LANES))[:, :COEF].astype(jnp.bfloat16)
    for o in range(8):
        child = lax.dot_general(parent, l2l_ref[o], NT, preferred_element_type=jnp.float32)
        level_one[o : o + 1, :] = pad_lanes(child)[:1]
    parents = level_one[...][:, :COEF].astype(jnp.bfloat16)
    for o in range(8):
        children = pad_lanes(lax.dot_general(parents, l2l_ref[o], NT, preferred_element_type=jnp.float32))
        for c in range(4):
            level_two[c, pl.ds(o, 8, stride=8), :] = children[:, c * 128 : (c + 1) * 128]

    def apply(weight, picked_ref):
        acc_ref[...] += lax.dot_general(
            weight, picked_value(picked_ref)[:, :COEF], NT, preferred_element_type=jnp.float32
        )

    acc_ref[...] = jnp.zeros_like(acc_ref)
    even_ref[...] = jnp.zeros_like(even_ref)

    def octant(o, carry):
        for c in range(4):
            rounded = level_two[c].astype(jnp.bfloat16).astype(jnp.float32)
            even_ref[pl.ds(c * 8 + o, BOX // 8, stride=32), :] = rounded
        apply(l2l_ref[o], even_ref)
        for c in range(4):
            even_ref[pl.ds(c * 8 + o, BOX // 8, stride=32), :] = jnp.zeros((BOX // 8, 128), jnp.float32)
        return carry

    lax.fori_loop(0, 8, octant, 0)

    for part in range(2):
        for n in range(4 * part, 4 * part + 4):
            @pl.when(exists(-DIR_SLAB[n], -DIR_SUB[n]))
            def _():
                ghost_copy(n).wait_recv()
        set_picked(odd_ref, ghost_in[4 * part : 4 * part + 4].reshape(BOX, LANES).astype(jnp.float32))
        spread_rows(odd_ref, table_ref, 1 + BOX + part * BOX)

    local[0].wait()
    local[2].wait()
    for step in range(1, AHEAD):
        forward(jnp.int32(0), jnp.int32(step))
        forward(jnp.int32(1), jnp.int32(step))

    def op_pair(i):
        step, carrier = i // 2, (core + i) % 2
        return (
            source(jnp.int32(0), carrier, step % 4, step // 4)[2],
            source(jnp.int32(1), carrier, step % 4, step // 4)[2],
        )

    def pick(k, picked_ref, unroll=True):
        pick_rows(lambda t: slot_ref[k, t] + 1, table_ref, picked_ref, unroll)

    pick(op_pair(jnp.int32(0))[0], even_ref, False)

    def main(i, carry):
        early, late = i // 2 + AHEAD, i // 2 + LATE

        @pl.when((early < 16) & jnp.logical_not(over_x(i % 2, early)))
        def _():
            forward(i % 2, early)

        @pl.when((late < 16) & over_x(i % 2, late))
        def _():
            forward(i % 2, late)

        k_even, k_odd = op_pair(i)
        k_next = op_pair(jnp.minimum(i + 1, 31))[0]

        @pl.when((i % 2 == 1) & (i > 1))
        def _():
            for k in (k_even, k_odd):
                pltpu.make_async_copy(ops_ref.at[k], ops_ref.at[k], op_recv.at[k]).wait()

        pick(k_odd, odd_ref)
        apply(ops_ref[k_even], even_ref)
        pick(k_next, even_ref)
        apply(ops_ref[k_odd], odd_ref)
        return carry

    lax.fori_loop(0, 32, main, 0)
    out_ref[...] = acc_ref[...].astype(out_ref.dtype)

    for cls in (0, 1):
        _, found = links(jnp.int32(cls), zero, zero, True)
        for kind in range(4):
            @pl.when(found[kind][0])
            def _():
                found[kind][1]().wait_send()

    def drain(i, carry):
        step = i // 2
        _, found = links(i % 2, step % 4, step // 4, False)
        for condition, copy in found:
            @pl.when(condition)
            def _():
                copy().wait_send()
        return carry

    lax.fori_loop(2, 32, drain, 0)
    for n in range(8):
        @pl.when(exists(DIR_SLAB[n], DIR_SUB[n]))
        def _():
            ghost_copy(n).wait_send()

    @pl.when(has_coarse)
    def _():
        for step in range(1, 8):
            coarse_copy(step).wait_send()


def shards(multipole, send_list, source_slot, m2l_ops, l2l_ops, coarse_exp):
    coarse = jnp.pad(coarse_exp, ((0, 0), (0, 112)))
    vmem = pl.BlockSpec(memory_space=pltpu.VMEM)
    smem = pl.BlockSpec(memory_space=pltpu.SMEM)
    hbm = pl.BlockSpec(memory_space=pltpu.HBM)
    f32, bf16 = jnp.float32, jnp.bfloat16
    return pl.pallas_call(
        kernel,
        out_shape=jax.ShapeDtypeStruct((COEF, BOX), bf16),
        in_specs=[vmem, smem, hbm, hbm, hbm, vmem],
        out_specs=vmem,
        scratch_shapes=[
            pltpu.SMEM((OFFSETS, BOX), jnp.int32),
            pltpu.VMEM((OFFSETS, COEF, COEF), bf16),
            pltpu.VMEM((8, COEF, COEF), bf16),
            pltpu.VMEM((COLS + 8, 4, 128), f32),
            pltpu.VMEM((BOX * 4, 128), f32),
            pltpu.VMEM((BOX * 4, 128), f32),
            pltpu.VMEM((COEF, BOX), f32),
            pltpu.VMEM((8, CAP, LANES), bf16),
            pltpu.VMEM((8, CAP, LANES), bf16),
            pltpu.VMEM((16, LANES), f32),
            pltpu.VMEM((8, LANES), f32),
            pltpu.VMEM((8, LANES), f32),
            pltpu.VMEM((4, 64, 128), f32),
            pltpu.SemaphoreType.DMA((3,)),
            pltpu.SemaphoreType.DMA((5, 32)),
            pltpu.SemaphoreType.DMA((OFFSETS,)),
            pltpu.SemaphoreType.DMA((8,)),
            pltpu.SemaphoreType.DMA((8,)),
            pltpu.SemaphoreType.DMA((7,)),
            pltpu.SemaphoreType.DMA,
        ],
        compiler_params=pltpu.CompilerParams(
            collective_id=0, has_side_effects=True, vmem_limit_bytes=60 * 2**20
        ),
        name="translate",
    )(multipole, send_list, source_slot, m2l_ops, l2l_ops, coarse)


def solution(mesh):
    placed = (
        P(None, ("slab", "sub")),
        P(("slab", "sub"), None, None),
        P(None, ("slab", "sub")),
        P("slab", None, None),
        P(),
        P(None, "sub"),
    )
    return jax.shard_map(
        shards, mesh=mesh, in_specs=placed, out_specs=P(None, ("slab", "sub")), check_vma=False
    )
```

```python
import jax
import jax.numpy as jnp
from jax import lax
from jax.experimental import pallas as pl
from jax.experimental.pallas import tpu as pltpu
from jax.sharding import PartitionSpec as P

DIR_SLAB = (-1, -1, -1, 0, 0, 1, 1, 1)
DIR_SUB = (-1, 0, 1, -1, 1, -1, 0, 1)
COEF, BOX, OFFSETS, CAP, COLS = 456, 512, 64, 128, 1536
LANES = 512
NT = (((1,), (1,)), ((), ()))
MESH = pl.DeviceIdType.MESH
HALF = 256
ROW, TILE = 5, 3
AHEAD = 4
LATE = 1
ORDER = (
    (0, 0), (1, 0), (2, 0), (0, 2), (0, 1), (3, 0), (1, 1), (2, 2),
    (1, 2), (2, 1), (0, 3), (3, 1), (1, 3), (2, 3), (3, 2), (3, 3),
)
SHARED = {(0, 1), (0, 2), (0, 3), (1, 0), (1, 2), (1, 3), (2, 0), (2, 2), (3, 0), (3, 2)}


def packed(digits, width):
    total = sum(d << (width * i) for i, d in enumerate(digits))
    return total - (1 << 32) if total >= 1 << 31 else total


FIRST = packed([q[0] for q in ORDER], 2)
SECOND = packed([q[1] for q in ORDER], 2)
SHARES = packed([(n % 4, n // 4) in SHARED for n in range(16)], 1)


def digit(code, place, width):
    return lax.shift_right_logical(jnp.int32(code), width * place) & (2**width - 1)


def node(step):
    step = jnp.clip(step, 0, 15)
    return digit(FIRST, step, 2), digit(SECOND, step, 2)


def shared(q1, q2):
    return digit(SHARES, q1 + 4 * q2, 1) == 1


def pick_rows(index_of, table_ref, picked_ref, unroll, first=0, count=BOX):
    def chunk(i, carry):
        for u in range(64):
            row = table_ref[index_of(i * 64 + u)]
            picked_ref[pl.ds(i * (64 * ROW) + u * ROW, 4, stride=TILE), :] = row
        return carry
    lax.fori_loop(first // 64, (first + count) // 64, chunk, 0, unroll=unroll)


def spread_rows(picked_ref, table_ref, first):
    def chunk(i, carry):
        for u in range(64):
            place = pl.ds(i * (64 * ROW) + u * ROW, 4, stride=TILE)
            table_ref[first + i * 64 + u] = picked_ref[place, :]
        return carry
    lax.fori_loop(0, BOX // 64, chunk, 0)


def picked_value(picked_ref, first=0, count=BOX):
    tiles = [picked_ref[pl.ds(ROW * first + TILE * c, count, stride=ROW), :] for c in range(4)]
    return jnp.concatenate(tiles, axis=1).astype(jnp.bfloat16)


def set_picked(picked_ref, rows):
    for c in range(4):
        picked_ref[pl.ds(TILE * c, BOX, stride=ROW), :] = rows[:, c * 128 : (c + 1) * 128]


def pad_lanes(rows):
    return jnp.concatenate([rows, jnp.zeros((rows.shape[0], LANES - COEF), rows.dtype)], axis=1)


def kernel(
    multipole_ref, send_list_ref, source_ref, ops_hbm, l2l_hbm, coarse_ref, out_ref,
    slot_vmem, slot_ref, ops_ref, l2l_ref, table_ref, even_ref, odd_ref, acc_ref, ghost_out, ghost_in,
    coarse_out, coarse_in, level_one, level_two,
    local_sem, op_send, op_recv, ghost_send, ghost_recv, coarse_send, coarse_recv,
):
    a, b = lax.axis_index("slab"), lax.axis_index("sub")
    z, y, x, core = a // 4, a % 4, b // 2, b % 2

    slot_vmem[...] = source_ref[...] + 1
    local = [
        pltpu.make_async_copy(slot_vmem, slot_ref, local_sem.at[0]),
        pltpu.make_async_copy(l2l_hbm, l2l_ref, local_sem.at[1]),
        pltpu.make_async_copy(ops_hbm, ops_ref.at[pl.ds(4 * a, 4)], local_sem.at[2]),
    ]
    for copy in local:
        copy.start()

    def exists(da, db):
        row, col = a + da, b + db
        return (row >= 0) & (row < 16) & (col >= 0) & (col < 8)

    ghost_in[...] = jnp.zeros_like(ghost_in)
    barrier = pltpu.get_barrier_semaphore()
    for step in range(1, 8):
        pl.semaphore_signal(barrier, inc=1, device_id=(a, (b + step) % 8), device_id_type=MESH)
    for dy, dz in ((1, 0), (3, 0), (0, 1), (0, 3)):
        there = ((z + dz) % 4) * 4 + (y + dy) % 4
        pl.semaphore_signal(barrier, inc=1, device_id=(there, b), device_id_type=MESH)
    greeted = 11
    for da, db in zip(DIR_SLAB, DIR_SUB):
        if da != 0:
            here = exists(da, db)

            @pl.when(here)
            def _():
                pl.semaphore_signal(barrier, inc=1, device_id=(a + da, b + db), device_id_type=MESH)

            greeted = greeted + here.astype(jnp.int32)

    pl.semaphore_wait(barrier, greeted)

    def source(cls, carrier, q1, q2):
        sign = 1 - 2 * carrier
        first = (q1 + (q1 == 2).astype(jnp.int32) - (q1 == 3).astype(jnp.int32)) * sign
        second = (q2 + (q2 == 2).astype(jnp.int32) - (q2 == 3).astype(jnp.int32)) * sign
        y0 = (y - jnp.where(cls == 0, first, second) + 4) % 4
        z0 = (z - jnp.where(cls == 0, second, first) + 4) % 4
        return y0, z0, 4 * (4 * z0 + y0) + 2 * carrier + cls

    sign = 1 - 2 * core

    def half(cls, y0, z0):
        return (x + y0 + z0 + cls) % 2 == 0

    def links(cls, q1, q2, own_op):
        y0, z0, k = source(cls, core, q1, q2)
        fed = half(cls, y0, z0)
        number = k // 4 * 2 + cls
        src = ops_hbm.at[2 * core + cls] if own_op else ops_ref.at[k]

        def goes(p1, p2):
            return fed | jnp.logical_not(shared(p1, p2))

        def copy(kind, device):
            return pltpu.make_async_remote_copy(
                src_ref=src, dst_ref=ops_ref.at[k], send_sem=op_send.at[kind, number],
                recv_sem=op_recv.at[k], device_id=device, device_id_type=MESH,
            )

        def along(axis_is_y, by):
            ny = jnp.where(axis_is_y, (y + by + 4) % 4, y)
            nz = jnp.where(axis_is_y, z, (z + by + 4) % 4)
            return (4 * nz + ny, b)

        prim_y = cls == 0
        beside = (a, ((x + sign + 4) % 4) * 2 + core)
        ahead = ((q1 == 0) & goes(1, 0)) | ((q1 == 1) & goes(3, 0))
        kinds = [
            ((q2 == 0) & ahead, lambda: copy(0, along(prim_y, sign))),
            ((q2 == 0) & (q1 == 0) & goes(2, 0), lambda: copy(1, along(prim_y, -sign))),
            (
                ((q2 == 0) & goes(q1, 1)) | ((q2 == 1) & goes(q1, 3)),
                lambda: copy(2, along(~prim_y, sign)),
            ),
            ((q2 == 0) & goes(q1, 2), lambda: copy(3, along(~prim_y, -sign))),
            (shared(q1, q2) & fed, lambda: copy(4, beside)),
            (q1 + q2 > 0, lambda: copy(5, (a, b + sign))),
        ]
        return k, kinds

    zero = jnp.int32(0)

    def start_own(cls, kinds):
        _, found = links(jnp.int32(cls), zero, zero, True)
        for kind in kinds:
            @pl.when(found[kind][0])
            def _():
                found[kind][1]().start()

    def over_x(cls, step):
        q1, q2 = node(step)
        y0, z0, _ = source(cls, core, q1, q2)
        return shared(q1, q2) & jnp.logical_not(half(cls, y0, z0))

    def forward(cls, step):
        k, found = links(cls, *node(step), False)
        pltpu.make_async_copy(ops_ref.at[k], ops_ref.at[k], op_recv.at[k]).wait()
        for condition, copy in found:
            @pl.when(condition)
            def _():
                copy().start()

    start_own(0, (0, 1))
    start_own(1, (0, 1))

    own = jnp.concatenate(
        [multipole_ref[...].astype(jnp.float32), jnp.zeros((LANES - COEF, BOX), jnp.float32)], axis=0
    ).T
    set_picked(even_ref, own)
    table_ref[0] = jnp.zeros((4, 128), jnp.float32)
    spread_rows(even_ref, table_ref, 1)
    coarse_out[...] = pad_lanes(coarse_ref[...].astype(jnp.float32))

    has_coarse = b == a // 2

    def coarse_copy(step):
        return pltpu.make_async_remote_copy(
            src_ref=coarse_out.at[pl.ds(pl.multiple_of(a % 2 * 8, 8), 8)], dst_ref=coarse_in,
            send_sem=coarse_send.at[step - 1], recv_sem=coarse_recv,
            device_id=(a, (b + step) % 8), device_id_type=MESH,
        )

    @pl.when(has_coarse)
    def _():
        for step in range(1, 8):
            coarse_copy(step).start()
        coarse_in[...] = coarse_out[pl.ds(pl.multiple_of(a % 2 * 8, 8), 8), :]

    def ghost_copy(n):
        da, db = DIR_SLAB[n], DIR_SUB[n]
        return pltpu.make_async_remote_copy(
            src_ref=ghost_out.at[n], dst_ref=ghost_in.at[n], send_sem=ghost_send.at[n],
            recv_sem=ghost_recv.at[n], device_id=(a + da, b + db), device_id_type=MESH,
        )

    for part in range(2):
        pick_rows(
            lambda t: jnp.maximum(send_list_ref[0, 4 * part + t // CAP, t % CAP], 0) + 1,
            table_ref, odd_ref, False,
        )
        ghost_out[4 * part : 4 * part + 4] = picked_value(odd_ref).reshape(4, CAP, LANES)
        for n in range(4 * part, 4 * part + 4):
            @pl.when(exists(DIR_SLAB[n], DIR_SUB[n]))
            def _():
                ghost_copy(n).start()

    start_own(0, (2, 3))
    start_own(1, (2, 3))

    @pl.when(jnp.logical_not(has_coarse))
    def _():
        coarse_copy(1).wait_recv()
    local[1].wait()

    parent = jnp.broadcast_to(coarse_in[pl.ds(b, 1), :], (8, LANES))[:, :COEF].astype(jnp.bfloat16)
    for o in range(8):
        child = lax.dot_general(parent, l2l_ref[o], NT, preferred_element_type=jnp.float32)
        level_one[o : o + 1, :] = pad_lanes(child)[:1]
    parents = level_one[...][:, :COEF].astype(jnp.bfloat16)
    for o in range(8):
        children = pad_lanes(lax.dot_general(parents, l2l_ref[o], NT, preferred_element_type=jnp.float32))
        for c in range(4):
            level_two[c, pl.ds(o, 8, stride=8), :] = children[:, c * 128 : (c + 1) * 128]

    def apply(weight, picked_ref, first=0, count=BOX):
        acc_ref[:, first : first + count] += lax.dot_general(
            weight, picked_value(picked_ref, first, count)[:, :COEF], NT,
            preferred_element_type=jnp.float32,
        )

    acc_ref[...] = jnp.zeros_like(acc_ref)
    even_ref[...] = jnp.zeros_like(even_ref)

    def octant(o, carry):
        early = (o - 8) // 2 + AHEAD

        @pl.when((early > 0) & jnp.logical_not(over_x(o % 2, early)))
        def _():
            forward(o % 2, early)

        for c in range(4):
            rounded = level_two[c].astype(jnp.bfloat16).astype(jnp.float32)
            even_ref[pl.ds(ROW * o + TILE * c, BOX // 8, stride=8 * ROW), :] = rounded
        apply(l2l_ref[o], even_ref)
        for c in range(4):
            even_ref[pl.ds(ROW * o + TILE * c, BOX // 8, stride=8 * ROW), :] = jnp.zeros((BOX // 8, 128), jnp.float32)
        return carry

    lax.fori_loop(0, 8, octant, 0)

    for part in range(2):
        for n in range(4 * part, 4 * part + 4):
            @pl.when(exists(-DIR_SLAB[n], -DIR_SUB[n]))
            def _():
                ghost_copy(n).wait_recv()
        set_picked(odd_ref, ghost_in[4 * part : 4 * part + 4].reshape(BOX, LANES).astype(jnp.float32))
        spread_rows(odd_ref, table_ref, 1 + BOX + part * BOX)

    local[0].wait()
    local[2].wait()
    def op_pair(i):
        step, carrier = i // 2, (core + i) % 2
        return (
            source(jnp.int32(0), carrier, *node(step))[2],
            source(jnp.int32(1), carrier, *node(step))[2],
        )

    def pick(k, picked_ref, unroll=True, first=0, count=BOX):
        pick_rows(lambda t: slot_ref[k, t], table_ref, picked_ref, unroll, first, count)

    def both(k_pick, pick_ref, k_apply, apply_ref):
        for first in range(0, BOX, HALF):
            pick(k_pick, pick_ref, True, first, HALF)
            apply(ops_ref[k_apply], apply_ref, first, HALF)

    pick(op_pair(jnp.int32(0))[0], even_ref, False)

    def main(i, carry):
        early, late = i // 2 + AHEAD, i // 2 + LATE

        @pl.when((early < 16) & jnp.logical_not(over_x(i % 2, early)))
        def _():
            forward(i % 2, early)

        @pl.when((late < 16) & over_x(i % 2, late))
        def _():
            forward(i % 2, late)

        k_even, k_odd = op_pair(i)
        k_next = op_pair(jnp.minimum(i + 1, 31))[0]

        @pl.when((i % 2 == 1) & (i > 1))
        def _():
            for k in (k_even, k_odd):
                pltpu.make_async_copy(ops_ref.at[k], ops_ref.at[k], op_recv.at[k]).wait()

        both(k_odd, odd_ref, k_even, even_ref)
        both(k_next, even_ref, k_odd, odd_ref)
        return carry

    lax.fori_loop(0, 32, main, 0)
    out_ref[...] = acc_ref[...].astype(out_ref.dtype)

    for cls in (0, 1):
        _, found = links(jnp.int32(cls), zero, zero, True)
        for kind in range(5):
            @pl.when(found[kind][0])
            def _():
                found[kind][1]().wait_send()

    def drain(i, carry):
        step = i // 2
        _, found = links(i % 2, *node(step), False)
        for condition, copy in found:
            @pl.when(condition)
            def _():
                copy().wait_send()
        return carry

    lax.fori_loop(2, 32, drain, 0)
    for n in range(8):
        @pl.when(exists(DIR_SLAB[n], DIR_SUB[n]))
        def _():
            ghost_copy(n).wait_send()

    @pl.when(has_coarse)
    def _():
        for step in range(1, 8):
            coarse_copy(step).wait_send()


def shards(multipole, send_list, source_slot, m2l_ops, l2l_ops, coarse_exp):
    vmem = pl.BlockSpec(memory_space=pltpu.VMEM)
    smem = pl.BlockSpec(memory_space=pltpu.SMEM)
    hbm = pl.BlockSpec(memory_space=pltpu.HBM)
    f32, bf16 = jnp.float32, jnp.bfloat16
    return pl.pallas_call(
        kernel,
        out_shape=jax.ShapeDtypeStruct((COEF, BOX), bf16),
        in_specs=[vmem, smem, vmem, hbm, hbm, vmem],
        out_specs=vmem,
        scratch_shapes=[
            pltpu.VMEM((OFFSETS, BOX), jnp.int32),
            pltpu.SMEM((OFFSETS, BOX), jnp.int32),
            pltpu.VMEM((OFFSETS, COEF, COEF), bf16),
            pltpu.VMEM((8, COEF, COEF), bf16),
            pltpu.VMEM((COLS + 8, 4, 128), f32),
            pltpu.VMEM((BOX * ROW + 16, 128), f32),
            pltpu.VMEM((BOX * ROW + 16, 128), f32),
            pltpu.VMEM((COEF, BOX), f32),
            pltpu.VMEM((8, CAP, LANES), bf16),
            pltpu.VMEM((8, CAP, LANES), bf16),
            pltpu.VMEM((16, LANES), f32),
            pltpu.VMEM((8, LANES), f32),
            pltpu.VMEM((8, LANES), f32),
            pltpu.VMEM((4, 64, 128), f32),
            pltpu.SemaphoreType.DMA((3,)),
            pltpu.SemaphoreType.DMA((6, 32)),
            pltpu.SemaphoreType.DMA((OFFSETS,)),
            pltpu.SemaphoreType.DMA((8,)),
            pltpu.SemaphoreType.DMA((8,)),
            pltpu.SemaphoreType.DMA((7,)),
            pltpu.SemaphoreType.DMA,
        ],
        compiler_params=pltpu.CompilerParams(
            collective_id=0, has_side_effects=True, vmem_limit_bytes=60 * 2**20
        ),
        name="translate",
    )(multipole, send_list, source_slot, m2l_ops, l2l_ops, coarse_exp.T)


def solution(mesh):
    placed = (
        P(None, ("slab", "sub")),
        P(("slab", "sub"), None, None),
        P(None, ("slab", "sub")),
        P("slab", None, None),
        P(),
        P(None, "sub"),
    )
    return jax.shard_map(
        shards, mesh=mesh, in_specs=placed, out_specs=P(None, ("slab", "sub")), check_vma=False
    )
```

```python
import jax
import jax.numpy as jnp
from jax import lax
from jax.experimental import pallas as pl
from jax.experimental.pallas import tpu as pltpu
from jax.sharding import PartitionSpec as P

DIR_SLAB = (-1, -1, -1, 0, 0, 1, 1, 1)
DIR_SUB = (-1, 0, 1, -1, 1, -1, 0, 1)
COEF, BOX, OFFSETS, CAP, COLS = 456, 512, 64, 128, 1536
LANES = 512
NT = (((1,), (1,)), ((), ()))
MESH = pl.DeviceIdType.MESH
HALF = 256
ROW, TILE = 5, 3
AHEAD = 4
LATE = 1
ORDER = (
    (0, 0), (1, 0), (2, 0), (0, 2), (0, 1), (3, 0), (1, 1), (2, 2),
    (1, 2), (2, 1), (0, 3), (3, 1), (1, 3), (2, 3), (3, 2), (3, 3),
)
SHARED = {(0, 1), (0, 2), (0, 3), (1, 0), (1, 2), (1, 3), (2, 0), (2, 2), (3, 0), (3, 2)}


def packed(digits, width):
    total = sum(d << (width * i) for i, d in enumerate(digits))
    return total - (1 << 32) if total >= 1 << 31 else total


FIRST = packed([q[0] for q in ORDER], 2)
SECOND = packed([q[1] for q in ORDER], 2)
SHARES = packed([(n % 4, n // 4) in SHARED for n in range(16)], 1)


def digit(code, place, width):
    return lax.shift_right_logical(jnp.int32(code), width * place) & (2**width - 1)


def node(step):
    step = jnp.clip(step, 0, 15)
    return digit(FIRST, step, 2), digit(SECOND, step, 2)


def shared(q1, q2):
    return digit(SHARES, q1 + 4 * q2, 1) == 1


def pick_rows(place_ref, table_ref, picked_ref, first=0, count=BOX):
    def chunk(i, carry):
        for u in range(64):
            row = table_ref[pl.ds(place_ref[i * 64 + u], 4), :]
            picked_ref[pl.ds(i * (64 * ROW) + u * ROW, 4, stride=TILE), :] = row
        return carry
    lax.fori_loop(first // 64, (first + count) // 64, chunk, 0, unroll=True)


def spread_rows(picked_ref, table_ref, first):
    def chunk(i, carry):
        for u in range(64):
            place = pl.ds(i * (64 * ROW) + u * ROW, 4, stride=TILE)
            table_ref[pl.ds(first * 4 + i * 256 + u * 4, 4), :] = picked_ref[place, :]
        return carry
    lax.fori_loop(0, BOX // 64, chunk, 0)


def picked_value(picked_ref, first=0, count=BOX):
    tiles = [picked_ref[pl.ds(ROW * first + TILE * c, count, stride=ROW), :] for c in range(4)]
    return jnp.concatenate(tiles, axis=1).astype(jnp.bfloat16)


def set_picked(picked_ref, rows):
    for c in range(4):
        picked_ref[pl.ds(TILE * c, BOX, stride=ROW), :] = rows[:, c * 128 : (c + 1) * 128]


def pad_lanes(rows):
    return jnp.concatenate([rows, jnp.zeros((rows.shape[0], LANES - COEF), rows.dtype)], axis=1)


def kernel(
    multipole_ref, send_list_ref, source_ref, ops_hbm, l2l_hbm, coarse_ref, out_ref,
    source_place, send_place, place_refs, ghost_places, ops_ref, l2l_ref, table_ref, even_ref, odd_ref, acc_ref, ghost_out, ghost_in,
    coarse_out, coarse_in, level_one, level_two,
    local_sem, place_sem, ghost_place_sem, op_send, op_recv, ghost_send, ghost_recv, coarse_send, coarse_recv,
):
    a, b = lax.axis_index("slab"), lax.axis_index("sub")
    z, y, x, core = a >> 2, a & 3, b >> 1, b & 1

    source_place[...] = (source_ref[...] + 1) * 4
    send_place[...] = (jnp.maximum(send_list_ref[0], 0) + 1) * 4
    local = [
        pltpu.make_async_copy(l2l_hbm, l2l_ref, local_sem.at[0]),
        pltpu.make_async_copy(ops_hbm, ops_ref.at[pl.ds(4 * a, 4)], local_sem.at[1]),
    ] + [
        pltpu.make_async_copy(
            send_place.at[n], ghost_places[n // 4].at[pl.ds(n % 4 * CAP, CAP)], ghost_place_sem.at[n]
        )
        for n in range(8)
    ]
    for copy in local:
        copy.start()

    def exists(da, db):
        row, col = a + da, b + db
        return (row >= 0) & (row < 16) & (col >= 0) & (col < 8)

    ghost_in[...] = jnp.zeros_like(ghost_in)
    barrier = pltpu.get_barrier_semaphore()
    for step in range(1, 8):
        pl.semaphore_signal(barrier, inc=1, device_id=(a, (b + step) % 8), device_id_type=MESH)
    for dy, dz in ((1, 0), (3, 0), (0, 1), (0, 3)):
        there = ((z + dz) % 4) * 4 + (y + dy) % 4
        pl.semaphore_signal(barrier, inc=1, device_id=(there, b), device_id_type=MESH)
    greeted = 11
    for da, db in zip(DIR_SLAB, DIR_SUB):
        if da != 0:
            here = exists(da, db)

            @pl.when(here)
            def _():
                pl.semaphore_signal(barrier, inc=1, device_id=(a + da, b + db), device_id_type=MESH)

            greeted = greeted + here.astype(jnp.int32)

    pl.semaphore_wait(barrier, greeted)

    def source(cls, carrier, q1, q2):
        sign = 1 - 2 * carrier
        first = (q1 ^ (q1 >> 1)) * sign
        second = (q2 ^ (q2 >> 1)) * sign
        y0 = (y - jnp.where(cls == 0, first, second)) & 3
        z0 = (z - jnp.where(cls == 0, second, first)) & 3
        return y0, z0, 16 * z0 + 4 * y0 + 2 * carrier + cls

    sign = 1 - 2 * core

    def half(cls, y0, z0):
        return (x + y0 + z0 + cls) & 1 == 0

    def links(cls, q1, q2, own_op):
        y0, z0, k = source(cls, core, q1, q2)
        fed = half(cls, y0, z0)
        number = (k >> 2) * 2 + cls
        src = ops_hbm.at[2 * core + cls] if own_op else ops_ref.at[k]

        def goes(p1, p2):
            return fed | jnp.logical_not(shared(p1, p2))

        def copy(kind, device):
            return pltpu.make_async_remote_copy(
                src_ref=src, dst_ref=ops_ref.at[k], send_sem=op_send.at[kind, number],
                recv_sem=op_recv.at[k], device_id=device, device_id_type=MESH,
            )

        def along(axis_is_y, by):
            ny = jnp.where(axis_is_y, (y + by) & 3, y)
            nz = jnp.where(axis_is_y, z, (z + by) & 3)
            return (4 * nz + ny, b)

        prim_y = cls == 0
        beside = (a, ((x + sign) & 3) * 2 + core)
        ahead = ((q1 == 0) & goes(1, 0)) | ((q1 == 1) & goes(3, 0))
        kinds = [
            ((q2 == 0) & ahead, lambda: copy(0, along(prim_y, sign))),
            ((q2 == 0) & (q1 == 0) & goes(2, 0), lambda: copy(1, along(prim_y, -sign))),
            (
                ((q2 == 0) & goes(q1, 1)) | ((q2 == 1) & goes(q1, 3)),
                lambda: copy(2, along(~prim_y, sign)),
            ),
            ((q2 == 0) & goes(q1, 2), lambda: copy(3, along(~prim_y, -sign))),
            (shared(q1, q2) & fed, lambda: copy(4, beside)),
            (q1 + q2 > 0, lambda: copy(5, (a, b + sign))),
        ]
        return k, kinds

    zero = jnp.int32(0)

    def start_own(cls, kinds):
        _, found = links(jnp.int32(cls), zero, zero, True)
        for kind in kinds:
            @pl.when(found[kind][0])
            def _():
                found[kind][1]().start()

    def over_x(cls, step):
        q1, q2 = node(step)
        y0, z0, _ = source(cls, core, q1, q2)
        return shared(q1, q2) & jnp.logical_not(half(cls, y0, z0))

    def forward(cls, step):
        k, found = links(cls, *node(step), False)
        pltpu.make_async_copy(ops_ref.at[k], ops_ref.at[k], op_recv.at[k]).wait()
        for condition, copy in found:
            @pl.when(condition)
            def _():
                copy().start()

    start_own(0, (0, 1))
    start_own(1, (0, 1))

    own = jnp.concatenate(
        [multipole_ref[...].astype(jnp.float32), jnp.zeros((LANES - COEF, BOX), jnp.float32)], axis=0
    ).T
    set_picked(even_ref, own)
    table_ref[0:4, :] = jnp.zeros((4, 128), jnp.float32)
    spread_rows(even_ref, table_ref, 1)
    coarse_out[...] = pad_lanes(coarse_ref[...].astype(jnp.float32))

    has_coarse = b == a // 2

    def coarse_copy(step):
        return pltpu.make_async_remote_copy(
            src_ref=coarse_out.at[pl.ds(pl.multiple_of(a % 2 * 8, 8), 8)], dst_ref=coarse_in,
            send_sem=coarse_send.at[step - 1], recv_sem=coarse_recv,
            device_id=(a, (b + step) % 8), device_id_type=MESH,
        )

    @pl.when(has_coarse)
    def _():
        for step in range(1, 8):
            coarse_copy(step).start()
        coarse_in[...] = coarse_out[pl.ds(pl.multiple_of(a % 2 * 8, 8), 8), :]

    def ghost_copy(n):
        da, db = DIR_SLAB[n], DIR_SUB[n]
        return pltpu.make_async_remote_copy(
            src_ref=ghost_out.at[n], dst_ref=ghost_in.at[n], send_sem=ghost_send.at[n],
            recv_sem=ghost_recv.at[n], device_id=(a + da, b + db), device_id_type=MESH,
        )

    for copy in local[2:]:
        copy.wait()
    for part in range(2):
        pick_rows(ghost_places[part], table_ref, odd_ref)
        ghost_out[4 * part : 4 * part + 4] = picked_value(odd_ref).reshape(4, CAP, LANES)
        for n in range(4 * part, 4 * part + 4):
            @pl.when(exists(DIR_SLAB[n], DIR_SUB[n]))
            def _():
                ghost_copy(n).start()

    start_own(0, (2, 3))
    start_own(1, (2, 3))

    @pl.when(jnp.logical_not(has_coarse))
    def _():
        coarse_copy(1).wait_recv()
    local[0].wait()

    parent = jnp.broadcast_to(coarse_in[pl.ds(b, 1), :], (8, LANES))[:, :COEF].astype(jnp.bfloat16)
    for o in range(8):
        child = lax.dot_general(parent, l2l_ref[o], NT, preferred_element_type=jnp.float32)
        level_one[o : o + 1, :] = pad_lanes(child)[:1]
    parents = level_one[...][:, :COEF].astype(jnp.bfloat16)
    for o in range(8):
        children = pad_lanes(lax.dot_general(parents, l2l_ref[o], NT, preferred_element_type=jnp.float32))
        for c in range(4):
            level_two[c, pl.ds(o, 8, stride=8), :] = children[:, c * 128 : (c + 1) * 128]

    def apply(weight, picked_ref, first=0, count=BOX):
        acc_ref[:, first : first + count] += lax.dot_general(
            weight, picked_value(picked_ref, first, count)[:, :COEF], NT,
            preferred_element_type=jnp.float32,
        )

    acc_ref[...] = jnp.zeros_like(acc_ref)
    even_ref[...] = jnp.zeros_like(even_ref)

    def octant(o, carry):
        early = (o - 8) // 2 + AHEAD

        @pl.when((early > 0) & jnp.logical_not(over_x(o % 2, early)))
        def _():
            forward(o % 2, early)

        for c in range(4):
            rounded = level_two[c].astype(jnp.bfloat16).astype(jnp.float32)
            even_ref[pl.ds(ROW * o + TILE * c, BOX // 8, stride=8 * ROW), :] = rounded
        apply(l2l_ref[o], even_ref)
        for c in range(4):
            even_ref[pl.ds(ROW * o + TILE * c, BOX // 8, stride=8 * ROW), :] = jnp.zeros((BOX // 8, 128), jnp.float32)
        return carry

    lax.fori_loop(0, 8, octant, 0)

    for part in range(2):
        for n in range(4 * part, 4 * part + 4):
            @pl.when(exists(-DIR_SLAB[n], -DIR_SUB[n]))
            def _():
                ghost_copy(n).wait_recv()
        set_picked(odd_ref, ghost_in[4 * part : 4 * part + 4].reshape(BOX, LANES).astype(jnp.float32))
        spread_rows(odd_ref, table_ref, 1 + BOX + part * BOX)

    local[1].wait()

    def ops_of(step):
        return [
            source(jnp.int32(cls), carrier, *node(step))[2]
            for carrier in (core, 1 - core) for cls in (0, 1)
        ]

    def place_copy(k, n):
        return pltpu.make_async_copy(source_place.at[k], place_refs[n], place_sem.at[n])

    def both(n_pick, pick_ref, k_apply, apply_ref):
        for first in range(0, BOX, HALF):
            pick_rows(place_refs[n_pick], table_ref, pick_ref, first, HALF)
            apply(ops_ref[k_apply], apply_ref, first, HALF)

    first_ops = ops_of(jnp.int32(0))
    for n in range(4):
        place_copy(first_ops[n], n).start()
    place_copy(first_ops[0], 0).wait()
    pick_rows(place_refs[0], table_ref, even_ref)
    place_copy(ops_of(jnp.int32(1))[0], 0).start()

    def main(step, carry):
        early, late = step + AHEAD, step + LATE

        def hand_on(cls):
            @pl.when((early < 16) & jnp.logical_not(over_x(cls, early)))
            def _():
                forward(cls, early)

            @pl.when((late < 16) & over_x(cls, late))
            def _():
                forward(cls, late)

        now, then = ops_of(step), ops_of(step + 1)
        after = ops_of(step + 2)
        hand_on(jnp.int32(0))
        place_copy(now[1], 1).wait()
        both(1, odd_ref, now[0], even_ref)

        @pl.when(step < 15)
        def _():
            place_copy(then[1], 1).start()

        hand_on(jnp.int32(1))
        place_copy(now[2], 2).wait()
        both(2, even_ref, now[1], odd_ref)

        @pl.when(step < 15)
        def _():
            place_copy(then[2], 2).start()

        @pl.when(step > 0)
        def _():
            for k in now[2:]:
                pltpu.make_async_copy(ops_ref.at[k], ops_ref.at[k], op_recv.at[k]).wait()

        place_copy(now[3], 3).wait()
        both(3, odd_ref, now[2], even_ref)

        @pl.when(step < 15)
        def _():
            place_copy(then[3], 3).start()
            place_copy(then[0], 0).wait()

        both(0, even_ref, now[3], odd_ref)

        @pl.when(step < 14)
        def _():
            place_copy(after[0], 0).start()

        return carry

    lax.fori_loop(0, 16, main, 0)
    out_ref[...] = acc_ref[...].astype(out_ref.dtype)

    for cls in (0, 1):
        _, found = links(jnp.int32(cls), zero, zero, True)
        for kind in range(5):
            @pl.when(found[kind][0])
            def _():
                found[kind][1]().wait_send()

    def drain(i, carry):
        step = i // 2
        _, found = links(i % 2, *node(step), False)
        for condition, copy in found:
            @pl.when(condition)
            def _():
                copy().wait_send()
        return carry

    lax.fori_loop(2, 32, drain, 0)
    for n in range(8):
        @pl.when(exists(DIR_SLAB[n], DIR_SUB[n]))
        def _():
            ghost_copy(n).wait_send()

    @pl.when(has_coarse)
    def _():
        for step in range(1, 8):
            coarse_copy(step).wait_send()


def shards(multipole, send_list, source_slot, m2l_ops, l2l_ops, coarse_exp):
    vmem = pl.BlockSpec(memory_space=pltpu.VMEM)
    hbm = pl.BlockSpec(memory_space=pltpu.HBM)
    f32, bf16 = jnp.float32, jnp.bfloat16
    return pl.pallas_call(
        kernel,
        out_shape=jax.ShapeDtypeStruct((COEF, BOX), bf16),
        in_specs=[vmem, vmem, vmem, hbm, hbm, vmem],
        out_specs=vmem,
        scratch_shapes=[
            pltpu.VMEM((OFFSETS, BOX), jnp.int32),
            pltpu.VMEM((8, CAP), jnp.int32),
            [pltpu.SMEM((BOX,), jnp.int32)] * 4,
            [pltpu.SMEM((BOX,), jnp.int32)] * 2,
            pltpu.VMEM((OFFSETS, COEF, COEF), bf16),
            pltpu.VMEM((8, COEF, COEF), bf16),
            pltpu.VMEM((4 * COLS + 32, 128), f32),
            pltpu.VMEM((BOX * ROW + 16, 128), f32),
            pltpu.VMEM((BOX * ROW + 16, 128), f32),
            pltpu.VMEM((COEF, BOX), f32),
            pltpu.VMEM((8, CAP, LANES), bf16),
            pltpu.VMEM((8, CAP, LANES), bf16),
            pltpu.VMEM((16, LANES), f32),
            pltpu.VMEM((8, LANES), f32),
            pltpu.VMEM((8, LANES), f32),
            pltpu.VMEM((4, 64, 128), f32),
            pltpu.SemaphoreType.DMA((2,)),
            pltpu.SemaphoreType.DMA((4,)),
            pltpu.SemaphoreType.DMA((8,)),
            pltpu.SemaphoreType.DMA((6, 32)),
            pltpu.SemaphoreType.DMA((OFFSETS,)),
            pltpu.SemaphoreType.DMA((8,)),
            pltpu.SemaphoreType.DMA((8,)),
            pltpu.SemaphoreType.DMA((7,)),
            pltpu.SemaphoreType.DMA,
        ],
        compiler_params=pltpu.CompilerParams(
            collective_id=0, has_side_effects=True, vmem_limit_bytes=60 * 2**20
        ),
        name="translate",
    )(multipole, send_list, source_slot, m2l_ops, l2l_ops, coarse_exp.T)


def solution(mesh):
    placed = (
        P(None, ("slab", "sub")),
        P(("slab", "sub"), None, None),
        P(None, ("slab", "sub")),
        P("slab", None, None),
        P(),
        P(None, "sub"),
    )
    return jax.shard_map(
        shards, mesh=mesh, in_specs=placed, out_specs=P(None, ("slab", "sub")), check_vma=False
    )
```

```python
import jax
import jax.numpy as jnp
from jax import lax
from jax.experimental import pallas as pl
from jax.experimental.pallas import tpu as pltpu
from jax.sharding import PartitionSpec as P

DIR_SLAB = (-1, -1, -1, 0, 0, 1, 1, 1)
DIR_SUB = (-1, 0, 1, -1, 1, -1, 0, 1)
COEF, BOX, OFFSETS, CAP, COLS = 456, 512, 64, 128, 1536
LANES = 512
NT = (((1,), (1,)), ((), ()))
MESH = pl.DeviceIdType.MESH
HALF = 256
ROW, TILE = 5, 3
AHEAD = 3
PARTS = ((0, 256), (256, COEF - 256))
LATE = 1
ORDER = (
    (0, 0), (1, 0), (2, 0), (0, 2), (0, 1), (3, 0), (1, 1), (2, 2),
    (1, 2), (2, 1), (0, 3), (3, 1), (1, 3), (2, 3), (3, 2), (3, 3),
)
SHARED = {(0, 1), (0, 2), (0, 3), (1, 0), (1, 2), (1, 3), (2, 0), (2, 2), (3, 0), (3, 2)}


def packed(digits, width):
    total = sum(d << (width * i) for i, d in enumerate(digits))
    return total - (1 << 32) if total >= 1 << 31 else total


FIRST = packed([q[0] for q in ORDER], 2)
SECOND = packed([q[1] for q in ORDER], 2)
SHARES = packed([(n % 4, n // 4) in SHARED for n in range(16)], 1)


def digit(code, place, width):
    return lax.shift_right_logical(jnp.int32(code), width * place) & (2**width - 1)


def node(step):
    step = jnp.clip(step, 0, 15)
    return digit(FIRST, step, 2), digit(SECOND, step, 2)


def shared(q1, q2):
    return digit(SHARES, q1 + 4 * q2, 1) == 1


def pick_rows(place_ref, table_ref, picked_ref, first=0, count=BOX):
    def chunk(i, carry):
        for u in range(64):
            row = table_ref[pl.ds(place_ref[i * 64 + u], 4), :]
            picked_ref[pl.ds(i * (64 * ROW) + u * ROW, 4, stride=TILE), :] = row
        return carry
    lax.fori_loop(first // 64, (first + count) // 64, chunk, 0, unroll=True)


def spread_rows(picked_ref, table_ref, first):
    def chunk(i, carry):
        for u in range(64):
            place = pl.ds(i * (64 * ROW) + u * ROW, 4, stride=TILE)
            table_ref[pl.ds(first * 4 + i * 256 + u * 4, 4), :] = picked_ref[place, :]
        return carry
    lax.fori_loop(0, BOX // 64, chunk, 0)


def picked_value(picked_ref, first=0, count=BOX):
    tiles = [picked_ref[pl.ds(ROW * first + TILE * c, count, stride=ROW), :] for c in range(4)]
    return jnp.concatenate(tiles, axis=1).astype(jnp.bfloat16)


def set_picked(picked_ref, rows):
    for c in range(4):
        picked_ref[pl.ds(TILE * c, BOX, stride=ROW), :] = rows[:, c * 128 : (c + 1) * 128]


def pad_lanes(rows):
    return jnp.concatenate([rows, jnp.zeros((rows.shape[0], LANES - COEF), rows.dtype)], axis=1)


def kernel(
    multipole_ref, send_list_ref, source_ref, ops_hbm, l2l_hbm, coarse_ref, out_ref,
    source_place, send_place, place_refs, ghost_places, ops_ref, l2l_ref, table_ref, even_ref, odd_ref, acc_ref, ghost_out, ghost_in,
    coarse_out, coarse_in, level_one, level_two,
    local_sem, place_sem, ghost_place_sem, op_send, op_recv, ghost_send, ghost_recv, coarse_send, coarse_recv,
):
    a, b = lax.axis_index("slab"), lax.axis_index("sub")
    z, y, x, core = a >> 2, a & 3, b >> 1, b & 1

    source_place[...] = (source_ref[...] + 1) * 4
    send_place[...] = (jnp.maximum(send_list_ref[0], 0) + 1) * 4
    local = [
        pltpu.make_async_copy(l2l_hbm, l2l_ref, local_sem.at[0]),
        pltpu.make_async_copy(ops_hbm, ops_ref.at[pl.ds(4 * a, 4)], local_sem.at[1]),
    ] + [
        pltpu.make_async_copy(
            send_place.at[n], ghost_places[n // 4].at[pl.ds(n % 4 * CAP, CAP)], ghost_place_sem.at[n]
        )
        for n in range(8)
    ]
    for copy in local:
        copy.start()

    def exists(da, db):
        row, col = a + da, b + db
        return (row >= 0) & (row < 16) & (col >= 0) & (col < 8)

    ghost_in[...] = jnp.zeros_like(ghost_in)
    barrier = pltpu.get_barrier_semaphore()
    for step in range(1, 8):
        pl.semaphore_signal(barrier, inc=1, device_id=(a, (b + step) % 8), device_id_type=MESH)
    for dy, dz in ((1, 0), (3, 0), (0, 1), (0, 3)):
        there = ((z + dz) % 4) * 4 + (y + dy) % 4
        pl.semaphore_signal(barrier, inc=1, device_id=(there, b), device_id_type=MESH)
    greeted = 11
    for da, db in zip(DIR_SLAB, DIR_SUB):
        if da != 0:
            here = exists(da, db)

            @pl.when(here)
            def _():
                pl.semaphore_signal(barrier, inc=1, device_id=(a + da, b + db), device_id_type=MESH)

            greeted = greeted + here.astype(jnp.int32)

    pl.semaphore_wait(barrier, greeted)

    def source(cls, carrier, q1, q2):
        sign = 1 - 2 * carrier
        first = (q1 ^ (q1 >> 1)) * sign
        second = (q2 ^ (q2 >> 1)) * sign
        y0 = (y - (second if cls & 1 else first)) & 3
        z0 = (z - (first if cls & 1 else second)) & 3
        return y0, z0, 16 * z0 + 4 * y0 + 2 * carrier + (cls & 1)

    sign = 1 - 2 * core

    def half(cls, y0, z0):
        return (x + y0 + z0 + cls + (cls >> 1)) & 1 == 0

    def links(cls, q1, q2, own_op):
        y0, z0, k = source(cls, core, q1, q2)
        fed = half(cls, y0, z0)
        number = (k >> 2) * 4 + cls
        lanes = pl.ds(*PARTS[cls >> 1])
        dst = ops_ref.at[k, :, lanes]
        src = ops_hbm.at[2 * core + (cls & 1), :, lanes] if own_op else dst

        def goes(p1, p2):
            return fed | jnp.logical_not(shared(p1, p2))

        def copy(kind, device):
            return pltpu.make_async_remote_copy(
                src_ref=src, dst_ref=dst, send_sem=op_send.at[kind, number],
                recv_sem=op_recv.at[cls >> 1, k], device_id=device, device_id_type=MESH,
            )

        def along(axis_is_y, by):
            return (4 * z + ((y + by) & 3), b) if axis_is_y else (4 * ((z + by) & 3) + y, b)

        prim_y = cls & 1 == 0
        beside = (a, ((x + sign) & 3) * 2 + core)
        ahead = ((q1 == 0) & goes(1, 0)) | ((q1 == 1) & goes(3, 0))
        kinds = [
            ((q2 == 0) & ahead, lambda: copy(0, along(prim_y, sign))),
            ((q2 == 0) & (q1 == 0) & goes(2, 0), lambda: copy(1, along(prim_y, -sign))),
            (
                ((q2 == 0) & goes(q1, 1)) | ((q2 == 1) & goes(q1, 3)),
                lambda: copy(2, along(not prim_y, sign)),
            ),
            ((q2 == 0) & goes(q1, 2), lambda: copy(3, along(not prim_y, -sign))),
            (shared(q1, q2) & fed, lambda: copy(4, beside)),
            (q1 + q2 > 0, lambda: copy(5, (a, b + sign))),
        ]
        return k, kinds

    zero = jnp.int32(0)

    def start_own(cls, kinds):
        _, found = links(cls, zero, zero, True)
        for kind in kinds:
            @pl.when(found[kind][0])
            def _():
                found[kind][1]().start()

    def over_x(cls, step):
        q1, q2 = node(step)
        y0, z0, _ = source(cls, core, q1, q2)
        return shared(q1, q2) & jnp.logical_not(half(cls, y0, z0))

    def arrive(k, part):
        here = ops_ref.at[k, :, pl.ds(*PARTS[part])]
        pltpu.make_async_copy(here, here, op_recv.at[part, k]).wait()

    def forward(cls, step):
        k, found = links(cls, *node(step), False)
        arrive(k, cls >> 1)
        for condition, copy in found:
            @pl.when(condition)
            def _():
                copy().start()

    for cls in range(4):
        start_own(cls, (0, 1))

    own = jnp.concatenate(
        [multipole_ref[...].astype(jnp.float32), jnp.zeros((LANES - COEF, BOX), jnp.float32)], axis=0
    ).T
    set_picked(even_ref, own)
    table_ref[0:4, :] = jnp.zeros((4, 128), jnp.float32)
    spread_rows(even_ref, table_ref, 1)
    coarse_out[...] = pad_lanes(coarse_ref[...].astype(jnp.float32))

    has_coarse = b == a // 2

    def coarse_copy(step):
        return pltpu.make_async_remote_copy(
            src_ref=coarse_out.at[pl.ds(pl.multiple_of(a % 2 * 8, 8), 8)], dst_ref=coarse_in,
            send_sem=coarse_send.at[step - 1], recv_sem=coarse_recv,
            device_id=(a, (b + step) % 8), device_id_type=MESH,
        )

    @pl.when(has_coarse)
    def _():
        for step in range(1, 8):
            coarse_copy(step).start()
        coarse_in[...] = coarse_out[pl.ds(pl.multiple_of(a % 2 * 8, 8), 8), :]

    def ghost_copy(n):
        da, db = DIR_SLAB[n], DIR_SUB[n]
        return pltpu.make_async_remote_copy(
            src_ref=ghost_out.at[n], dst_ref=ghost_in.at[n], send_sem=ghost_send.at[n],
            recv_sem=ghost_recv.at[n], device_id=(a + da, b + db), device_id_type=MESH,
        )

    for copy in local[2:]:
        copy.wait()
    for part in range(2):
        pick_rows(ghost_places[part], table_ref, odd_ref)
        ghost_out[4 * part : 4 * part + 4] = picked_value(odd_ref).reshape(4, CAP, LANES)
        for n in range(4 * part, 4 * part + 4):
            @pl.when(exists(DIR_SLAB[n], DIR_SUB[n]))
            def _():
                ghost_copy(n).start()

    for cls in range(4):
        start_own(cls, (2, 3))

    @pl.when(jnp.logical_not(has_coarse))
    def _():
        coarse_copy(1).wait_recv()
    local[0].wait()

    parent = jnp.broadcast_to(coarse_in[pl.ds(b, 1), :], (8, LANES))[:, :COEF].astype(jnp.bfloat16)
    for o in range(8):
        child = lax.dot_general(parent, l2l_ref[o], NT, preferred_element_type=jnp.float32)
        level_one[o : o + 1, :] = pad_lanes(child)[:1]
    parents = level_one[...][:, :COEF].astype(jnp.bfloat16)
    for o in range(8):
        children = pad_lanes(lax.dot_general(parents, l2l_ref[o], NT, preferred_element_type=jnp.float32))
        for c in range(4):
            level_two[c, pl.ds(o, 8, stride=8), :] = children[:, c * 128 : (c + 1) * 128]

    def apply(weight, picked_ref, first=0, count=BOX):
        acc_ref[:, first : first + count] += lax.dot_general(
            weight, picked_value(picked_ref, first, count)[:, :COEF], NT,
            preferred_element_type=jnp.float32,
        )

    acc_ref[...] = jnp.zeros_like(acc_ref)
    even_ref[...] = jnp.zeros_like(even_ref)

    def hand_on(cls, step):
        early, late = step + AHEAD, step + LATE

        @pl.when((early < 16) & jnp.logical_not(over_x(cls, early)))
        def _():
            forward(cls, early)

        @pl.when((late > 0) & (late < 16) & over_x(cls, late))
        def _():
            forward(cls, late)

    def octants(i, carry):
        for cls in range(4):
            o = 4 * i + cls
            hand_on(cls, i - 2)
            for c in range(4):
                rounded = level_two[c].astype(jnp.bfloat16).astype(jnp.float32)
                even_ref[pl.ds(ROW * o + TILE * c, BOX // 8, stride=8 * ROW), :] = rounded
            apply(l2l_ref[o], even_ref)
            for c in range(4):
                even_ref[pl.ds(ROW * o + TILE * c, BOX // 8, stride=8 * ROW), :] = jnp.zeros(
                    (BOX // 8, 128), jnp.float32
                )
        return carry

    lax.fori_loop(0, 2, octants, 0)

    for part in range(2):
        for n in range(4 * part, 4 * part + 4):
            @pl.when(exists(-DIR_SLAB[n], -DIR_SUB[n]))
            def _():
                ghost_copy(n).wait_recv()
        set_picked(odd_ref, ghost_in[4 * part : 4 * part + 4].reshape(BOX, LANES).astype(jnp.float32))
        spread_rows(odd_ref, table_ref, 1 + BOX + part * BOX)

    local[1].wait()

    def ops_of(step):
        return [
            source(cls, carrier, *node(step))[2]
            for carrier in (core, 1 - core) for cls in (0, 1)
        ]

    def place_copy(k, n):
        return pltpu.make_async_copy(source_place.at[k], place_refs[n], place_sem.at[n])

    def both(n_pick, pick_ref, k_apply, apply_ref):
        for first in range(0, BOX, HALF):
            pick_rows(place_refs[n_pick], table_ref, pick_ref, first, HALF)
            apply(ops_ref[k_apply], apply_ref, first, HALF)

    first_ops = ops_of(jnp.int32(0))
    for n in range(4):
        place_copy(first_ops[n], n).start()
    place_copy(first_ops[0], 0).wait()
    pick_rows(place_refs[0], table_ref, even_ref)
    place_copy(ops_of(jnp.int32(1))[0], 0).start()

    def main(step, carry):
        now, then = ops_of(step), ops_of(step + 1)
        after = ops_of(step + 2)
        hand_on(0, step)
        place_copy(now[1], 1).wait()
        both(1, odd_ref, now[0], even_ref)

        @pl.when(step < 15)
        def _():
            place_copy(then[1], 1).start()

        hand_on(1, step)
        place_copy(now[2], 2).wait()
        both(2, even_ref, now[1], odd_ref)

        @pl.when(step < 15)
        def _():
            place_copy(then[2], 2).start()

        hand_on(2, step)

        @pl.when(step > 0)
        def _():
            for k in now[2:]:
                arrive(k, 0)
                arrive(k, 1)

        place_copy(now[3], 3).wait()
        both(3, odd_ref, now[2], even_ref)

        @pl.when(step < 15)
        def _():
            place_copy(then[3], 3).start()
            place_copy(then[0], 0).wait()

        hand_on(3, step)
        both(0, even_ref, now[3], odd_ref)

        @pl.when(step < 14)
        def _():
            place_copy(after[0], 0).start()

        return carry

    lax.fori_loop(0, 16, main, 0)
    out_ref[...] = acc_ref[...].astype(out_ref.dtype)

    for cls in range(4):
        _, found = links(cls, zero, zero, True)
        for kind in range(5):
            @pl.when(found[kind][0])
            def _():
                found[kind][1]().wait_send()

    def drain(step, carry):
        for cls in range(4):
            _, found = links(cls, *node(step), False)
            for condition, copy in found:
                @pl.when(condition)
                def _():
                    copy().wait_send()
        return carry

    lax.fori_loop(1, 16, drain, 0)
    for n in range(8):
        @pl.when(exists(DIR_SLAB[n], DIR_SUB[n]))
        def _():
            ghost_copy(n).wait_send()

    @pl.when(has_coarse)
    def _():
        for step in range(1, 8):
            coarse_copy(step).wait_send()


def shards(multipole, send_list, source_slot, m2l_ops, l2l_ops, coarse_exp):
    vmem = pl.BlockSpec(memory_space=pltpu.VMEM)
    hbm = pl.BlockSpec(memory_space=pltpu.HBM)
    f32, bf16 = jnp.float32, jnp.bfloat16
    return pl.pallas_call(
        kernel,
        out_shape=jax.ShapeDtypeStruct((COEF, BOX), bf16),
        in_specs=[vmem, vmem, vmem, hbm, hbm, vmem],
        out_specs=vmem,
        scratch_shapes=[
            pltpu.VMEM((OFFSETS, BOX), jnp.int32),
            pltpu.VMEM((8, CAP), jnp.int32),
            [pltpu.SMEM((BOX,), jnp.int32)] * 4,
            [pltpu.SMEM((BOX,), jnp.int32)] * 2,
            pltpu.VMEM((OFFSETS, COEF, COEF), bf16),
            pltpu.VMEM((8, COEF, COEF), bf16),
            pltpu.VMEM((4 * COLS + 32, 128), f32),
            pltpu.VMEM((BOX * ROW + 16, 128), f32),
            pltpu.VMEM((BOX * ROW + 16, 128), f32),
            pltpu.VMEM((COEF, BOX), f32),
            pltpu.VMEM((8, CAP, LANES), bf16),
            pltpu.VMEM((8, CAP, LANES), bf16),
            pltpu.VMEM((16, LANES), f32),
            pltpu.VMEM((8, LANES), f32),
            pltpu.VMEM((8, LANES), f32),
            pltpu.VMEM((4, 64, 128), f32),
            pltpu.SemaphoreType.DMA((2,)),
            pltpu.SemaphoreType.DMA((4,)),
            pltpu.SemaphoreType.DMA((8,)),
            pltpu.SemaphoreType.DMA((6, 64)),
            pltpu.SemaphoreType.DMA((2, OFFSETS)),
            pltpu.SemaphoreType.DMA((8,)),
            pltpu.SemaphoreType.DMA((8,)),
            pltpu.SemaphoreType.DMA((7,)),
            pltpu.SemaphoreType.DMA,
        ],
        compiler_params=pltpu.CompilerParams(
            collective_id=0, has_side_effects=True, vmem_limit_bytes=60 * 2**20
        ),
        name="translate",
    )(multipole, send_list, source_slot, m2l_ops, l2l_ops, coarse_exp.T)


def solution(mesh):
    placed = (
        P(None, ("slab", "sub")),
        P(("slab", "sub"), None, None),
        P(None, ("slab", "sub")),
        P("slab", None, None),
        P(),
        P(None, "sub"),
    )
    return jax.shard_map(
        shards, mesh=mesh, in_specs=placed, out_specs=P(None, ("slab", "sub")), check_vma=False
    )
```

```python
import jax
import jax.numpy as jnp
from jax import lax
from jax.experimental import pallas as pl
from jax.experimental.pallas import tpu as pltpu
from jax.sharding import PartitionSpec as P

DIR_SLAB = (-1, -1, -1, 0, 0, 1, 1, 1)
DIR_SUB = (-1, 0, 1, -1, 1, -1, 0, 1)
COEF, BOX, OFFSETS, CAP, COLS = 456, 512, 64, 128, 1536
LANES = 512
NT = (((1,), (1,)), ((), ()))
MESH = pl.DeviceIdType.MESH
HALF = 256
ROW, TILE = 5, 3
AHEAD = 3
PARTS = ((0, 224), (224, COEF - 224))
LATE = 1
ORDER = (
    (0, 0), (1, 0), (2, 0), (0, 2), (0, 1), (3, 0), (1, 1), (2, 2),
    (1, 2), (2, 1), (0, 3), (3, 1), (1, 3), (2, 3), (3, 2), (3, 3),
)
SHARED = {(0, 1), (0, 2), (0, 3), (1, 0), (1, 2), (1, 3), (2, 0), (2, 2), (3, 0), (3, 2)}


def packed(digits, width):
    total = sum(d << (width * i) for i, d in enumerate(digits))
    return total - (1 << 32) if total >= 1 << 31 else total


FIRST = packed([q[0] for q in ORDER], 2)
SECOND = packed([q[1] for q in ORDER], 2)
SHARES = packed([(n % 4, n // 4) in SHARED for n in range(16)], 1)


def digit(code, place, width):
    return lax.shift_right_logical(jnp.int32(code), width * place) & (2**width - 1)


def node(step):
    step = jnp.clip(step, 0, 15)
    return digit(FIRST, step, 2), digit(SECOND, step, 2)


def shared(q1, q2):
    return digit(SHARES, q1 + 4 * q2, 1) == 1


def pick_rows(place_ref, table_ref, picked_ref, first=0, count=BOX):
    def chunk(i, carry):
        for u in range(64):
            row = table_ref[pl.ds(place_ref[i * 64 + u], 4), :]
            picked_ref[pl.ds(i * (64 * ROW) + u * ROW, 4, stride=TILE), :] = row
        return carry
    lax.fori_loop(first // 64, (first + count) // 64, chunk, 0, unroll=True)


def spread_rows(picked_ref, table_ref, first):
    def chunk(i, carry):
        for u in range(64):
            place = pl.ds(i * (64 * ROW) + u * ROW, 4, stride=TILE)
            table_ref[pl.ds(first * 4 + i * 256 + u * 4, 4), :] = picked_ref[place, :]
        return carry
    lax.fori_loop(0, BOX // 64, chunk, 0)


def picked_value(picked_ref, first=0, count=BOX):
    tiles = [picked_ref[pl.ds(ROW * first + TILE * c, count, stride=ROW), :] for c in range(4)]
    return jnp.concatenate(tiles, axis=1).astype(jnp.bfloat16)


def set_picked(picked_ref, rows):
    for c in range(4):
        picked_ref[pl.ds(TILE * c, BOX, stride=ROW), :] = rows[:, c * 128 : (c + 1) * 128]


def pad_lanes(rows):
    return jnp.concatenate([rows, jnp.zeros((rows.shape[0], LANES - COEF), rows.dtype)], axis=1)


def kernel(
    multipole_ref, send_list_ref, source_ref, ops_hbm, l2l_hbm, coarse_ref, out_ref,
    source_place, send_place, place_refs, ghost_places, ops_ref, l2l_ref, table_ref, even_ref, odd_ref, acc_ref, ghost_out, ghost_in,
    coarse_out, coarse_in, level_one, level_two,
    local_sem, place_sem, ghost_place_sem, op_send, op_recv, ghost_send, ghost_recv, coarse_send, coarse_recv,
):
    a, b = lax.axis_index("slab"), lax.axis_index("sub")
    z, y, x, core = a >> 2, a & 3, b >> 1, b & 1

    source_place[...] = (source_ref[...] + 1) * 4
    send_place[...] = (jnp.maximum(send_list_ref[0], 0) + 1) * 4
    local = [
        pltpu.make_async_copy(l2l_hbm, l2l_ref, local_sem.at[0]),
        pltpu.make_async_copy(ops_hbm, ops_ref.at[pl.ds(4 * a, 4)], local_sem.at[1]),
    ] + [
        pltpu.make_async_copy(
            send_place.at[n], ghost_places[n // 4].at[pl.ds(n % 4 * CAP, CAP)], ghost_place_sem.at[n]
        )
        for n in range(8)
    ]
    for copy in local:
        copy.start()

    def exists(da, db):
        row, col = a + da, b + db
        return (row >= 0) & (row < 16) & (col >= 0) & (col < 8)

    ghost_in[...] = jnp.zeros_like(ghost_in)
    barrier = pltpu.get_barrier_semaphore()
    for step in range(1, 8):
        pl.semaphore_signal(barrier, inc=1, device_id=(a, (b + step) % 8), device_id_type=MESH)
    for dy, dz in ((1, 0), (3, 0), (0, 1), (0, 3)):
        there = ((z + dz) % 4) * 4 + (y + dy) % 4
        pl.semaphore_signal(barrier, inc=1, device_id=(there, b), device_id_type=MESH)
    greeted = 11
    for da, db in zip(DIR_SLAB, DIR_SUB):
        if da != 0:
            here = exists(da, db)

            @pl.when(here)
            def _():
                pl.semaphore_signal(barrier, inc=1, device_id=(a + da, b + db), device_id_type=MESH)

            greeted = greeted + here.astype(jnp.int32)

    pl.semaphore_wait(barrier, greeted)

    def source(cls, carrier, q1, q2):
        sign = 1 - 2 * carrier
        first = (q1 ^ (q1 >> 1)) * sign
        second = (q2 ^ (q2 >> 1)) * sign
        y0 = (y - (second if cls & 1 else first)) & 3
        z0 = (z - (first if cls & 1 else second)) & 3
        return y0, z0, 16 * z0 + 4 * y0 + 2 * carrier + (cls & 1)

    sign = 1 - 2 * core

    def half(cls, y0, z0):
        return (x + y0 + z0 + cls + (cls >> 1)) & 1 == 0

    def links(cls, q1, q2, own_op):
        y0, z0, k = source(cls, core, q1, q2)
        fed = half(cls, y0, z0)
        number = (k >> 2) * 4 + cls
        rows = pl.ds(*PARTS[cls >> 1])
        dst = ops_ref.at[k, rows]
        src = ops_hbm.at[2 * core + (cls & 1), rows] if own_op else dst

        def goes(p1, p2):
            return fed | jnp.logical_not(shared(p1, p2))

        def copy(kind, device):
            return pltpu.make_async_remote_copy(
                src_ref=src, dst_ref=dst, send_sem=op_send.at[kind, number],
                recv_sem=op_recv.at[cls >> 1, k], device_id=device, device_id_type=MESH,
            )

        def along(axis_is_y, by):
            return (4 * z + ((y + by) & 3), b) if axis_is_y else (4 * ((z + by) & 3) + y, b)

        prim_y = cls & 1 == 0
        beside = (a, ((x + sign) & 3) * 2 + core)
        ahead = ((q1 == 0) & goes(1, 0)) | ((q1 == 1) & goes(3, 0))
        kinds = [
            ((q2 == 0) & ahead, lambda: copy(0, along(prim_y, sign))),
            ((q2 == 0) & (q1 == 0) & goes(2, 0), lambda: copy(1, along(prim_y, -sign))),
            (
                ((q2 == 0) & goes(q1, 1)) | ((q2 == 1) & goes(q1, 3)),
                lambda: copy(2, along(not prim_y, sign)),
            ),
            ((q2 == 0) & goes(q1, 2), lambda: copy(3, along(not prim_y, -sign))),
            (shared(q1, q2) & fed, lambda: copy(4, beside)),
            (q1 + q2 > 0, lambda: copy(5, (a, b + sign))),
        ]
        return k, kinds

    zero = jnp.int32(0)

    def start_own(cls, kinds):
        _, found = links(cls, zero, zero, True)
        for kind in kinds:
            @pl.when(found[kind][0])
            def _():
                found[kind][1]().start()

    def over_x(cls, step):
        q1, q2 = node(step)
        y0, z0, _ = source(cls, core, q1, q2)
        return shared(q1, q2) & jnp.logical_not(half(cls, y0, z0))

    def arrive(k, part):
        here = ops_ref.at[k, pl.ds(*PARTS[part])]
        pltpu.make_async_copy(here, here, op_recv.at[part, k]).wait()

    def forward(cls, step):
        k, found = links(cls, *node(step), False)
        arrive(k, cls >> 1)
        for condition, copy in found:
            @pl.when(condition)
            def _():
                copy().start()

    for cls in range(4):
        start_own(cls, (0, 1))

    own = jnp.concatenate(
        [multipole_ref[...].astype(jnp.float32), jnp.zeros((LANES - COEF, BOX), jnp.float32)], axis=0
    ).T
    set_picked(even_ref, own)
    table_ref[0:4, :] = jnp.zeros((4, 128), jnp.float32)
    spread_rows(even_ref, table_ref, 1)
    coarse_out[...] = pad_lanes(coarse_ref[...].astype(jnp.float32))

    has_coarse = b == a // 2

    def coarse_copy(step):
        return pltpu.make_async_remote_copy(
            src_ref=coarse_out.at[pl.ds(pl.multiple_of(a % 2 * 8, 8), 8)], dst_ref=coarse_in,
            send_sem=coarse_send.at[step - 1], recv_sem=coarse_recv,
            device_id=(a, (b + step) % 8), device_id_type=MESH,
        )

    @pl.when(has_coarse)
    def _():
        for step in range(1, 8):
            coarse_copy(step).start()
        coarse_in[...] = coarse_out[pl.ds(pl.multiple_of(a % 2 * 8, 8), 8), :]

    def ghost_copy(n):
        da, db = DIR_SLAB[n], DIR_SUB[n]
        return pltpu.make_async_remote_copy(
            src_ref=ghost_out.at[n], dst_ref=ghost_in.at[n], send_sem=ghost_send.at[n],
            recv_sem=ghost_recv.at[n], device_id=(a + da, b + db), device_id_type=MESH,
        )

    for copy in local[2:]:
        copy.wait()
    for part in range(2):
        pick_rows(ghost_places[part], table_ref, odd_ref)
        ghost_out[4 * part : 4 * part + 4] = picked_value(odd_ref).reshape(4, CAP, LANES)
        for n in range(4 * part, 4 * part + 4):
            @pl.when(exists(DIR_SLAB[n], DIR_SUB[n]))
            def _():
                ghost_copy(n).start()

    for cls in range(4):
        start_own(cls, (2, 3))

    @pl.when(jnp.logical_not(has_coarse))
    def _():
        coarse_copy(1).wait_recv()
    local[0].wait()

    parent = jnp.broadcast_to(coarse_in[pl.ds(b, 1), :], (8, LANES))[:, :COEF].astype(jnp.bfloat16)
    for o in range(8):
        child = lax.dot_general(parent, l2l_ref[o], NT, preferred_element_type=jnp.float32)
        level_one[o : o + 1, :] = pad_lanes(child)[:1]
    parents = level_one[...][:, :COEF].astype(jnp.bfloat16)
    for o in range(8):
        children = pad_lanes(lax.dot_general(parents, l2l_ref[o], NT, preferred_element_type=jnp.float32))
        for c in range(4):
            level_two[c, pl.ds(o, 8, stride=8), :] = children[:, c * 128 : (c + 1) * 128]

    def apply(weight, picked_ref, first=0, count=BOX):
        acc_ref[:, first : first + count] += lax.dot_general(
            weight, picked_value(picked_ref, first, count)[:, :COEF], NT,
            preferred_element_type=jnp.float32,
        )

    acc_ref[...] = jnp.zeros_like(acc_ref)
    even_ref[...] = jnp.zeros_like(even_ref)

    def hand_on(cls, step):
        early, late = step + AHEAD, step + LATE

        @pl.when((early < 16) & jnp.logical_not(over_x(cls, early)))
        def _():
            forward(cls, early)

        @pl.when((late > 0) & (late < 16) & over_x(cls, late))
        def _():
            forward(cls, late)

    def octants(i, carry):
        for cls in range(4):
            o = 4 * i + cls
            hand_on(cls, i - 2)
            for c in range(4):
                rounded = level_two[c].astype(jnp.bfloat16).astype(jnp.float32)
                even_ref[pl.ds(ROW * o + TILE * c, BOX // 8, stride=8 * ROW), :] = rounded
            apply(l2l_ref[o], even_ref)
            for c in range(4):
                even_ref[pl.ds(ROW * o + TILE * c, BOX // 8, stride=8 * ROW), :] = jnp.zeros(
                    (BOX // 8, 128), jnp.float32
                )
        return carry

    lax.fori_loop(0, 2, octants, 0)

    for part in range(2):
        for n in range(4 * part, 4 * part + 4):
            @pl.when(exists(-DIR_SLAB[n], -DIR_SUB[n]))
            def _():
                ghost_copy(n).wait_recv()
        set_picked(odd_ref, ghost_in[4 * part : 4 * part + 4].reshape(BOX, LANES).astype(jnp.float32))
        spread_rows(odd_ref, table_ref, 1 + BOX + part * BOX)

    local[1].wait()

    def ops_of(step):
        return [
            source(cls, carrier, *node(step))[2]
            for carrier in (core, 1 - core) for cls in (0, 1)
        ]

    def place_copy(k, n):
        return pltpu.make_async_copy(source_place.at[k], place_refs[n], place_sem.at[n])

    def both(n_pick, pick_ref, k_apply, apply_ref):
        for first in range(0, BOX, HALF):
            pick_rows(place_refs[n_pick], table_ref, pick_ref, first, HALF)
            apply(ops_ref[k_apply], apply_ref, first, HALF)

    first_ops = ops_of(jnp.int32(0))
    for n in range(4):
        place_copy(first_ops[n], n).start()
    place_copy(first_ops[0], 0).wait()
    pick_rows(place_refs[0], table_ref, even_ref)
    place_copy(ops_of(jnp.int32(1))[0], 0).start()

    def main(step, carry):
        now, then = ops_of(step), ops_of(step + 1)
        after = ops_of(step + 2)
        hand_on(0, step)
        place_copy(now[1], 1).wait()
        both(1, odd_ref, now[0], even_ref)

        @pl.when(step < 15)
        def _():
            place_copy(then[1], 1).start()

        hand_on(1, step)
        place_copy(now[2], 2).wait()
        both(2, even_ref, now[1], odd_ref)

        @pl.when(step < 15)
        def _():
            place_copy(then[2], 2).start()

        hand_on(2, step)

        @pl.when(step > 0)
        def _():
            for k in now[2:]:
                arrive(k, 0)
                arrive(k, 1)

        place_copy(now[3], 3).wait()
        both(3, odd_ref, now[2], even_ref)

        @pl.when(step < 15)
        def _():
            place_copy(then[3], 3).start()
            place_copy(then[0], 0).wait()

        hand_on(3, step)
        both(0, even_ref, now[3], odd_ref)

        @pl.when(step < 14)
        def _():
            place_copy(after[0], 0).start()

        return carry

    lax.fori_loop(0, 16, main, 0)
    out_ref[...] = acc_ref[...].astype(out_ref.dtype)

    for cls in range(4):
        _, found = links(cls, zero, zero, True)
        for kind in range(5):
            @pl.when(found[kind][0])
            def _():
                found[kind][1]().wait_send()

    def drain(step, carry):
        for cls in range(4):
            _, found = links(cls, *node(step), False)
            for condition, copy in found:
                @pl.when(condition)
                def _():
                    copy().wait_send()
        return carry

    lax.fori_loop(1, 16, drain, 0)
    for n in range(8):
        @pl.when(exists(DIR_SLAB[n], DIR_SUB[n]))
        def _():
            ghost_copy(n).wait_send()

    @pl.when(has_coarse)
    def _():
        for step in range(1, 8):
            coarse_copy(step).wait_send()


def shards(multipole, send_list, source_slot, m2l_ops, l2l_ops, coarse_exp):
    vmem = pl.BlockSpec(memory_space=pltpu.VMEM)
    hbm = pl.BlockSpec(memory_space=pltpu.HBM)
    f32, bf16 = jnp.float32, jnp.bfloat16
    return pl.pallas_call(
        kernel,
        out_shape=jax.ShapeDtypeStruct((COEF, BOX), bf16),
        in_specs=[vmem, vmem, vmem, hbm, hbm, vmem],
        out_specs=vmem,
        scratch_shapes=[
            pltpu.VMEM((OFFSETS, BOX), jnp.int32),
            pltpu.VMEM((8, CAP), jnp.int32),
            [pltpu.SMEM((BOX,), jnp.int32)] * 4,
            [pltpu.SMEM((BOX,), jnp.int32)] * 2,
            pltpu.VMEM((OFFSETS, COEF, COEF), bf16),
            pltpu.VMEM((8, COEF, COEF), bf16),
            pltpu.VMEM((4 * COLS + 32, 128), f32),
            pltpu.VMEM((BOX * ROW + 16, 128), f32),
            pltpu.VMEM((BOX * ROW + 16, 128), f32),
            pltpu.VMEM((COEF, BOX), f32),
            pltpu.VMEM((8, CAP, LANES), bf16),
            pltpu.VMEM((8, CAP, LANES), bf16),
            pltpu.VMEM((16, LANES), f32),
            pltpu.VMEM((8, LANES), f32),
            pltpu.VMEM((8, LANES), f32),
            pltpu.VMEM((4, 64, 128), f32),
            pltpu.SemaphoreType.DMA((2,)),
            pltpu.SemaphoreType.DMA((4,)),
            pltpu.SemaphoreType.DMA((8,)),
            pltpu.SemaphoreType.DMA((6, 64)),
            pltpu.SemaphoreType.DMA((2, OFFSETS)),
            pltpu.SemaphoreType.DMA((8,)),
            pltpu.SemaphoreType.DMA((8,)),
            pltpu.SemaphoreType.DMA((7,)),
            pltpu.SemaphoreType.DMA,
        ],
        compiler_params=pltpu.CompilerParams(
            collective_id=0, has_side_effects=True, vmem_limit_bytes=60 * 2**20
        ),
        name="translate",
    )(multipole, send_list, source_slot, m2l_ops, l2l_ops, coarse_exp.T)


def solution(mesh):
    placed = (
        P(None, ("slab", "sub")),
        P(("slab", "sub"), None, None),
        P(None, ("slab", "sub")),
        P("slab", None, None),
        P(),
        P(None, "sub"),
    )
    return jax.shard_map(
        shards, mesh=mesh, in_specs=placed, out_specs=P(None, ("slab", "sub")), check_vma=False
    )
```

```python
import jax
import jax.numpy as jnp
from jax import lax
from jax.experimental import pallas as pl
from jax.experimental.pallas import tpu as pltpu
from jax.sharding import PartitionSpec as P

DIR_SLAB = (-1, -1, -1, 0, 0, 1, 1, 1)
DIR_SUB = (-1, 0, 1, -1, 1, -1, 0, 1)
COEF, BOX, OFFSETS, CAP, COLS = 456, 512, 64, 128, 1536
LANES = 512
NT = (((1,), (1,)), ((), ()))
MESH = pl.DeviceIdType.MESH
HALF = 256
ROW, TILE = 5, 3
AHEAD = 4
LATE = 1
ORDER = (
    (0, 0), (1, 0), (2, 0), (0, 2), (0, 1), (3, 0), (1, 2), (1, 1),
    (0, 3), (2, 2), (2, 1), (3, 1), (3, 2), (1, 3), (2, 3), (3, 3),
)
SHARED = {(0, 1), (0, 2), (0, 3), (1, 2), (1, 3), (2, 0), (2, 2), (3, 0), (3, 2)}


def packed(digits, width):
    total = sum(d << (width * i) for i, d in enumerate(digits))
    return total - (1 << 32) if total >= 1 << 31 else total


FIRST = packed([q[0] for q in ORDER], 2)
SECOND = packed([q[1] for q in ORDER], 2)
SHARES = packed([(n % 4, n // 4) in SHARED for n in range(16)], 1)


def digit(code, place, width):
    return lax.shift_right_logical(jnp.int32(code), width * place) & (2**width - 1)


def node(step):
    step = jnp.clip(step, 0, 15)
    return digit(FIRST, step, 2), digit(SECOND, step, 2)


def shared(q1, q2):
    return digit(SHARES, q1 + 4 * q2, 1) == 1


def pick_rows(place_ref, table_ref, picked_ref, first=0, count=BOX):
    def chunk(i, carry):
        for u in range(64):
            row = table_ref[pl.ds(place_ref[i * 64 + u], 4), :]
            picked_ref[pl.ds(i * (64 * ROW) + u * ROW, 4, stride=TILE), :] = row
        return carry
    lax.fori_loop(first // 64, (first + count) // 64, chunk, 0, unroll=True)


def spread_rows(picked_ref, table_ref, first):
    def chunk(i, carry):
        for u in range(64):
            place = pl.ds(i * (64 * ROW) + u * ROW, 4, stride=TILE)
            table_ref[pl.ds(first * 4 + i * 256 + u * 4, 4), :] = picked_ref[place, :]
        return carry
    lax.fori_loop(0, BOX // 64, chunk, 0)


def picked_value(picked_ref, first=0, count=BOX):
    tiles = [picked_ref[pl.ds(ROW * first + TILE * c, count, stride=ROW), :] for c in range(4)]
    return jnp.concatenate(tiles, axis=1).astype(jnp.bfloat16)


def set_picked(picked_ref, rows):
    for c in range(4):
        picked_ref[pl.ds(TILE * c, BOX, stride=ROW), :] = rows[:, c * 128 : (c + 1) * 128]


def pad_lanes(rows):
    return jnp.concatenate([rows, jnp.zeros((rows.shape[0], LANES - COEF), rows.dtype)], axis=1)


def kernel(
    multipole_ref, send_list_ref, source_ref, ops_hbm, l2l_hbm, coarse_ref, out_ref,
    source_place, send_place, place_refs, ghost_places, ops_ref, l2l_ref, table_ref, even_ref, odd_ref, acc_ref, ghost_out, ghost_in,
    coarse_out, coarse_in, level_one, level_two,
    local_sem, place_sem, ghost_place_sem, op_send, op_recv, ghost_send, ghost_recv, coarse_send, coarse_recv,
):
    a, b = lax.axis_index("slab"), lax.axis_index("sub")
    z, y, x, core = a >> 2, a & 3, b >> 1, b & 1

    source_place[...] = (source_ref[...] + 1) * 4
    send_place[...] = (jnp.maximum(send_list_ref[0], 0) + 1) * 4
    local = [
        pltpu.make_async_copy(l2l_hbm, l2l_ref, local_sem.at[0]),
        pltpu.make_async_copy(ops_hbm, ops_ref.at[pl.ds(4 * a, 4)], local_sem.at[1]),
    ] + [
        pltpu.make_async_copy(
            send_place.at[n], ghost_places[n // 4].at[pl.ds(n % 4 * CAP, CAP)], ghost_place_sem.at[n]
        )
        for n in range(8)
    ]
    for copy in local:
        copy.start()

    def exists(da, db):
        row, col = a + da, b + db
        return (row >= 0) & (row < 16) & (col >= 0) & (col < 8)

    ghost_in[...] = jnp.zeros_like(ghost_in)
    barrier = pltpu.get_barrier_semaphore()
    for step in range(1, 8):
        pl.semaphore_signal(barrier, inc=1, device_id=(a, (b + step) % 8), device_id_type=MESH)
    for dy, dz in ((1, 0), (3, 0), (0, 1), (0, 3)):
        there = ((z + dz) % 4) * 4 + (y + dy) % 4
        pl.semaphore_signal(barrier, inc=1, device_id=(there, b), device_id_type=MESH)
    greeted = 11
    for da, db in zip(DIR_SLAB, DIR_SUB):
        if da != 0:
            here = exists(da, db)

            @pl.when(here)
            def _():
                pl.semaphore_signal(barrier, inc=1, device_id=(a + da, b + db), device_id_type=MESH)

            greeted = greeted + here.astype(jnp.int32)

    pl.semaphore_wait(barrier, greeted)

    def source(cls, carrier, q1, q2):
        sign = 1 - 2 * carrier
        first = (q1 ^ (q1 >> 1)) * sign
        second = (q2 ^ (q2 >> 1)) * sign
        y0 = (y - jnp.where(cls == 0, first, second)) & 3
        z0 = (z - jnp.where(cls == 0, second, first)) & 3
        return y0, z0, 16 * z0 + 4 * y0 + 2 * carrier + cls

    sign = 1 - 2 * core

    def half(cls, y0, z0):
        return (x + y0 + z0 + cls) & 1 == 0

    def links(cls, q1, q2, own_op):
        y0, z0, k = source(cls, core, q1, q2)
        fed = half(cls, y0, z0)
        number = (k >> 2) * 2 + cls
        src = ops_hbm.at[2 * core + cls] if own_op else ops_ref.at[k]

        def goes(p1, p2):
            return fed | jnp.logical_not(shared(p1, p2))

        def copy(kind, device):
            return pltpu.make_async_remote_copy(
                src_ref=src, dst_ref=ops_ref.at[k], send_sem=op_send.at[kind, number],
                recv_sem=op_recv.at[k], device_id=device, device_id_type=MESH,
            )

        def along(axis_is_y, by):
            ny = jnp.where(axis_is_y, (y + by) & 3, y)
            nz = jnp.where(axis_is_y, z, (z + by) & 3)
            return (4 * nz + ny, b)

        prim_y = cls == 0
        beside = (a, ((x + sign) & 3) * 2 + core)
        ahead = ((q1 == 0) & goes(1, 0)) | ((q1 == 1) & goes(3, 0))
        kinds = [
            ((q2 == 0) & ahead, lambda: copy(0, along(prim_y, sign))),
            ((q2 == 0) & (q1 == 0) & goes(2, 0), lambda: copy(1, along(prim_y, -sign))),
            (
                ((q2 == 0) & goes(q1, 1)) | ((q2 == 1) & goes(q1, 3)),
                lambda: copy(2, along(~prim_y, sign)),
            ),
            ((q2 == 0) & goes(q1, 2), lambda: copy(3, along(~prim_y, -sign))),
            (shared(q1, q2) & fed, lambda: copy(4, beside)),
            (q1 + q2 > 0, lambda: copy(5, (a, b + sign))),
        ]
        return k, kinds

    zero = jnp.int32(0)

    def start_own(cls, kinds):
        _, found = links(jnp.int32(cls), zero, zero, True)
        for kind in kinds:
            @pl.when(found[kind][0])
            def _():
                found[kind][1]().start()

    def over_x(cls, step):
        q1, q2 = node(step)
        y0, z0, _ = source(cls, core, q1, q2)
        return shared(q1, q2) & jnp.logical_not(half(cls, y0, z0))

    def forward(cls, step):
        k, found = links(cls, *node(step), False)
        pltpu.make_async_copy(ops_ref.at[k], ops_ref.at[k], op_recv.at[k]).wait()
        for condition, copy in found:
            @pl.when(condition)
            def _():
                copy().start()

    start_own(0, (0, 1))
    start_own(1, (0, 1))

    own = jnp.concatenate(
        [multipole_ref[...].astype(jnp.float32), jnp.zeros((LANES - COEF, BOX), jnp.float32)], axis=0
    ).T
    set_picked(even_ref, own)
    table_ref[0:4, :] = jnp.zeros((4, 128), jnp.float32)
    spread_rows(even_ref, table_ref, 1)
    coarse_out[...] = pad_lanes(coarse_ref[...].astype(jnp.float32))

    has_coarse = b == a // 2

    def coarse_copy(step):
        return pltpu.make_async_remote_copy(
            src_ref=coarse_out.at[pl.ds(pl.multiple_of(a % 2 * 8, 8), 8)], dst_ref=coarse_in,
            send_sem=coarse_send.at[step - 1], recv_sem=coarse_recv,
            device_id=(a, (b + step) % 8), device_id_type=MESH,
        )

    @pl.when(has_coarse)
    def _():
        for step in range(1, 8):
            coarse_copy(step).start()
        coarse_in[...] = coarse_out[pl.ds(pl.multiple_of(a % 2 * 8, 8), 8), :]

    def ghost_copy(n):
        da, db = DIR_SLAB[n], DIR_SUB[n]
        return pltpu.make_async_remote_copy(
            src_ref=ghost_out.at[n], dst_ref=ghost_in.at[n], send_sem=ghost_send.at[n],
            recv_sem=ghost_recv.at[n], device_id=(a + da, b + db), device_id_type=MESH,
        )

    for copy in local[2:]:
        copy.wait()
    for part in range(2):
        pick_rows(ghost_places[part], table_ref, odd_ref)
        ghost_out[4 * part : 4 * part + 4] = picked_value(odd_ref).reshape(4, CAP, LANES)
        for n in range(4 * part, 4 * part + 4):
            @pl.when(exists(DIR_SLAB[n], DIR_SUB[n]))
            def _():
                ghost_copy(n).start()

    start_own(0, (2, 3))
    start_own(1, (2, 3))

    @pl.when(jnp.logical_not(has_coarse))
    def _():
        coarse_copy(1).wait_recv()
    local[0].wait()

    parent = jnp.broadcast_to(coarse_in[pl.ds(b, 1), :], (8, LANES))[:, :COEF].astype(jnp.bfloat16)
    for o in range(8):
        child = lax.dot_general(parent, l2l_ref[o], NT, preferred_element_type=jnp.float32)
        level_one[o : o + 1, :] = pad_lanes(child)[:1]
    parents = level_one[...][:, :COEF].astype(jnp.bfloat16)
    for o in range(8):
        children = pad_lanes(lax.dot_general(parents, l2l_ref[o], NT, preferred_element_type=jnp.float32))
        for c in range(4):
            level_two[c, pl.ds(o, 8, stride=8), :] = children[:, c * 128 : (c + 1) * 128]

    def apply(weight, picked_ref, first=0, count=BOX):
        acc_ref[:, first : first + count] += lax.dot_general(
            weight, picked_value(picked_ref, first, count)[:, :COEF], NT,
            preferred_element_type=jnp.float32,
        )

    acc_ref[...] = jnp.zeros_like(acc_ref)
    even_ref[...] = jnp.zeros_like(even_ref)

    def octant(o, carry):
        early = (o - 8) // 2 + AHEAD

        @pl.when((early > 0) & jnp.logical_not(over_x(o % 2, early)))
        def _():
            forward(o % 2, early)

        for c in range(4):
            rounded = level_two[c].astype(jnp.bfloat16).astype(jnp.float32)
            even_ref[pl.ds(ROW * o + TILE * c, BOX // 8, stride=8 * ROW), :] = rounded
        apply(l2l_ref[o], even_ref)
        for c in range(4):
            even_ref[pl.ds(ROW * o + TILE * c, BOX // 8, stride=8 * ROW), :] = jnp.zeros((BOX // 8, 128), jnp.float32)
        return carry

    lax.fori_loop(0, 8, octant, 0)

    for part in range(2):
        for n in range(4 * part, 4 * part + 4):
            @pl.when(exists(-DIR_SLAB[n], -DIR_SUB[n]))
            def _():
                ghost_copy(n).wait_recv()
        set_picked(odd_ref, ghost_in[4 * part : 4 * part + 4].reshape(BOX, LANES).astype(jnp.float32))
        spread_rows(odd_ref, table_ref, 1 + BOX + part * BOX)

    local[1].wait()

    def ops_of(step):
        return [
            source(jnp.int32(cls), carrier, *node(step))[2]
            for carrier in (core, 1 - core) for cls in (0, 1)
        ]

    def place_copy(k, n):
        return pltpu.make_async_copy(source_place.at[k], place_refs[n], place_sem.at[n])

    def both(n_pick, pick_ref, k_apply, apply_ref):
        for first in range(0, BOX, HALF):
            pick_rows(place_refs[n_pick], table_ref, pick_ref, first, HALF)
            apply(ops_ref[k_apply], apply_ref, first, HALF)

    first_ops = ops_of(jnp.int32(0))
    for n in range(4):
        place_copy(first_ops[n], n).start()
    place_copy(first_ops[0], 0).wait()
    pick_rows(place_refs[0], table_ref, even_ref)
    place_copy(ops_of(jnp.int32(1))[0], 0).start()

    def main(step, carry):
        early, late = step + AHEAD, step + LATE

        def hand_on(cls):
            @pl.when((early < 16) & jnp.logical_not(over_x(cls, early)))
            def _():
                forward(cls, early)

            @pl.when((late < 16) & over_x(cls, late))
            def _():
                forward(cls, late)

        now, then = ops_of(step), ops_of(step + 1)
        after = ops_of(step + 2)
        hand_on(jnp.int32(0))
        place_copy(now[1], 1).wait()
        both(1, odd_ref, now[0], even_ref)

        @pl.when(step < 15)
        def _():
            place_copy(then[1], 1).start()

        hand_on(jnp.int32(1))
        place_copy(now[2], 2).wait()
        both(2, even_ref, now[1], odd_ref)

        @pl.when(step < 15)
        def _():
            place_copy(then[2], 2).start()

        @pl.when(step > 0)
        def _():
            for k in now[2:]:
                pltpu.make_async_copy(ops_ref.at[k], ops_ref.at[k], op_recv.at[k]).wait()

        place_copy(now[3], 3).wait()
        both(3, odd_ref, now[2], even_ref)

        @pl.when(step < 15)
        def _():
            place_copy(then[3], 3).start()
            place_copy(then[0], 0).wait()

        both(0, even_ref, now[3], odd_ref)

        @pl.when(step < 14)
        def _():
            place_copy(after[0], 0).start()

        return carry

    lax.fori_loop(0, 16, main, 0)
    out_ref[...] = acc_ref[...].astype(out_ref.dtype)

    for cls in (0, 1):
        _, found = links(jnp.int32(cls), zero, zero, True)
        for kind in range(5):
            @pl.when(found[kind][0])
            def _():
                found[kind][1]().wait_send()

    def drain(i, carry):
        step = i // 2
        _, found = links(i % 2, *node(step), False)
        for condition, copy in found:
            @pl.when(condition)
            def _():
                copy().wait_send()
        return carry

    lax.fori_loop(2, 32, drain, 0)
    for n in range(8):
        @pl.when(exists(DIR_SLAB[n], DIR_SUB[n]))
        def _():
            ghost_copy(n).wait_send()

    @pl.when(has_coarse)
    def _():
        for step in range(1, 8):
            coarse_copy(step).wait_send()


def shards(multipole, send_list, source_slot, m2l_ops, l2l_ops, coarse_exp):
    vmem = pl.BlockSpec(memory_space=pltpu.VMEM)
    hbm = pl.BlockSpec(memory_space=pltpu.HBM)
    f32, bf16 = jnp.float32, jnp.bfloat16
    return pl.pallas_call(
        kernel,
        out_shape=jax.ShapeDtypeStruct((COEF, BOX), bf16),
        in_specs=[vmem, vmem, vmem, hbm, hbm, vmem],
        out_specs=vmem,
        scratch_shapes=[
            pltpu.VMEM((OFFSETS, BOX), jnp.int32),
            pltpu.VMEM((8, CAP), jnp.int32),
            [pltpu.SMEM((BOX,), jnp.int32)] * 4,
            [pltpu.SMEM((BOX,), jnp.int32)] * 2,
            pltpu.VMEM((OFFSETS, COEF, COEF), bf16),
            pltpu.VMEM((8, COEF, COEF), bf16),
            pltpu.VMEM((4 * COLS + 32, 128), f32),
            pltpu.VMEM((BOX * ROW + 16, 128), f32),
            pltpu.VMEM((BOX * ROW + 16, 128), f32),
            pltpu.VMEM((COEF, BOX), f32),
            pltpu.VMEM((8, CAP, LANES), bf16),
            pltpu.VMEM((8, CAP, LANES), bf16),
            pltpu.VMEM((16, LANES), f32),
            pltpu.VMEM((8, LANES), f32),
            pltpu.VMEM((8, LANES), f32),
            pltpu.VMEM((4, 64, 128), f32),
            pltpu.SemaphoreType.DMA((2,)),
            pltpu.SemaphoreType.DMA((4,)),
            pltpu.SemaphoreType.DMA((8,)),
            pltpu.SemaphoreType.DMA((6, 32)),
            pltpu.SemaphoreType.DMA((OFFSETS,)),
            pltpu.SemaphoreType.DMA((8,)),
            pltpu.SemaphoreType.DMA((8,)),
            pltpu.SemaphoreType.DMA((7,)),
            pltpu.SemaphoreType.DMA,
        ],
        compiler_params=pltpu.CompilerParams(
            collective_id=0, has_side_effects=True, vmem_limit_bytes=60 * 2**20
        ),
        name="translate",
    )(multipole, send_list, source_slot, m2l_ops, l2l_ops, coarse_exp.T)


def solution(mesh):
    placed = (
        P(None, ("slab", "sub")),
        P(("slab", "sub"), None, None),
        P(None, ("slab", "sub")),
        P("slab", None, None),
        P(),
        P(None, "sub"),
    )
    return jax.shard_map(
        shards, mesh=mesh, in_specs=placed, out_specs=P(None, ("slab", "sub")), check_vma=False
    )
```

```python
import jax
import jax.numpy as jnp
from jax import lax
from jax.experimental import pallas as pl
from jax.experimental.pallas import tpu as pltpu
from jax.sharding import PartitionSpec as P

DIR_SLAB = (-1, -1, -1, 0, 0, 1, 1, 1)
DIR_SUB = (-1, 0, 1, -1, 1, -1, 0, 1)
COEF, BOX, OFFSETS, CAP, COLS = 456, 512, 64, 128, 1536
LANES = 512
NT = (((1,), (1,)), ((), ()))
MESH = pl.DeviceIdType.MESH
HALF = 256
ROW, TILE = 5, 3
AHEAD = 4
SENT = 60
LATE = 1
ORDER = (
    (0, 0), (1, 0), (2, 0), (0, 2), (0, 1), (3, 0), (1, 1), (2, 2),
    (1, 2), (2, 1), (0, 3), (3, 1), (1, 3), (2, 3), (3, 2), (3, 3),
)
SHARED = {(0, 1), (0, 2), (0, 3), (1, 0), (1, 2), (1, 3), (2, 0), (2, 2), (3, 0), (3, 2)}


def packed(digits, width):
    total = sum(d << (width * i) for i, d in enumerate(digits))
    return total - (1 << 32) if total >= 1 << 31 else total


FIRST = packed([q[0] for q in ORDER], 2)
SECOND = packed([q[1] for q in ORDER], 2)
SHARES = packed([(n % 4, n // 4) in SHARED for n in range(16)], 1)


def digit(code, place, width):
    return lax.shift_right_logical(jnp.int32(code), width * place) & (2**width - 1)


def node(step):
    step = jnp.clip(step, 0, 15)
    return digit(FIRST, step, 2), digit(SECOND, step, 2)


def shared(q1, q2):
    return digit(SHARES, q1 + 4 * q2, 1) == 1


def pick_rows(place_ref, table_ref, picked_ref, first=0, count=BOX):
    def chunk(i, carry):
        for u in range(64):
            row = table_ref[pl.ds(place_ref[i * 64 + u], 4), :]
            picked_ref[pl.ds(i * (64 * ROW) + u * ROW, 4, stride=TILE), :] = row
        return carry
    lax.fori_loop(first // 64, (first + count) // 64, chunk, 0, unroll=True)


def spread_rows(picked_ref, table_ref, first):
    def chunk(i, carry):
        for u in range(64):
            place = pl.ds(i * (64 * ROW) + u * ROW, 4, stride=TILE)
            table_ref[pl.ds(first * 4 + i * 256 + u * 4, 4), :] = picked_ref[place, :]
        return carry
    lax.fori_loop(0, BOX // 64, chunk, 0)


def picked_value(picked_ref, first=0, count=BOX):
    tiles = [picked_ref[pl.ds(ROW * first + TILE * c, count, stride=ROW), :] for c in range(4)]
    return jnp.concatenate(tiles, axis=1).astype(jnp.bfloat16)


def set_picked(picked_ref, rows):
    for c in range(4):
        picked_ref[pl.ds(TILE * c, BOX, stride=ROW), :] = rows[:, c * 128 : (c + 1) * 128]


def pad_lanes(rows):
    return jnp.concatenate([rows, jnp.zeros((rows.shape[0], LANES - COEF), rows.dtype)], axis=1)


def kernel(
    multipole_ref, send_list_ref, source_ref, ops_hbm, l2l_hbm, coarse_ref, out_ref,
    source_place, send_place, place_refs, ghost_places, ops_ref, l2l_ref, table_ref, even_ref, odd_ref, acc_ref, ghost_out, ghost_in,
    coarse_out, coarse_in, level_one, level_two,
    local_sem, place_sem, ghost_place_sem, op_send, op_recv, ghost_send, ghost_recv, coarse_send, coarse_recv,
):
    a, b = lax.axis_index("slab"), lax.axis_index("sub")
    z, y, x, core = a >> 2, a & 3, b >> 1, b & 1

    def exists(da, db):
        row, col = a + da, b + db
        return (row >= 0) & (row < 16) & (col >= 0) & (col < 8)

    ghost_in[...] = jnp.zeros_like(ghost_in)
    barrier = pltpu.get_barrier_semaphore()
    for step in range(1, 8):
        pl.semaphore_signal(barrier, inc=1, device_id=(a, (b + step) % 8), device_id_type=MESH)
    for dy, dz in ((1, 0), (3, 0), (0, 1), (0, 3)):
        there = ((z + dz) % 4) * 4 + (y + dy) % 4
        pl.semaphore_signal(barrier, inc=1, device_id=(there, b), device_id_type=MESH)
    greeted = 11
    for da, db in zip(DIR_SLAB, DIR_SUB):
        if da != 0:
            here = exists(da, db)

            @pl.when(here)
            def _():
                pl.semaphore_signal(barrier, inc=1, device_id=(a + da, b + db), device_id_type=MESH)

            greeted = greeted + here.astype(jnp.int32)

    source_place[...] = (source_ref[...] + 1) * 4
    send_place[...] = (jnp.maximum(send_list_ref[0], 0) + 1) * 4
    local = [
        pltpu.make_async_copy(l2l_hbm, l2l_ref, local_sem.at[0]),
        pltpu.make_async_copy(ops_hbm, ops_ref.at[pl.ds(4 * a, 4)], local_sem.at[1]),
    ] + [
        pltpu.make_async_copy(
            send_place.at[n], ghost_places[n // 4].at[pl.ds(n % 4 * CAP, CAP)], ghost_place_sem.at[n]
        )
        for n in range(8)
    ]
    for copy in local:
        copy.start()

    pl.semaphore_wait(barrier, greeted)

    def source(cls, carrier, q1, q2):
        sign = 1 - 2 * carrier
        first = (q1 ^ (q1 >> 1)) * sign
        second = (q2 ^ (q2 >> 1)) * sign
        y0 = (y - jnp.where(cls == 0, first, second)) & 3
        z0 = (z - jnp.where(cls == 0, second, first)) & 3
        return y0, z0, 16 * z0 + 4 * y0 + 2 * carrier + cls

    sign = 1 - 2 * core

    def half(cls, y0, z0):
        return (x + y0 + z0 + cls) & 1 == 0

    def links(cls, q1, q2, own_op):
        y0, z0, k = source(cls, core, q1, q2)
        fed = half(cls, y0, z0)
        src = ops_hbm.at[2 * core + cls] if own_op else ops_ref.at[k]

        def goes(p1, p2):
            return fed | jnp.logical_not(shared(p1, p2))

        def copy(device):
            return pltpu.make_async_remote_copy(
                src_ref=src, dst_ref=ops_ref.at[k], send_sem=op_send,
                recv_sem=op_recv.at[k], device_id=device, device_id_type=MESH,
            )

        def along(axis_is_y, by):
            ny = jnp.where(axis_is_y, (y + by) & 3, y)
            nz = jnp.where(axis_is_y, z, (z + by) & 3)
            return (4 * nz + ny, b)

        prim_y = cls == 0
        beside = (a, ((x + sign) & 3) * 2 + core)
        ahead = ((q1 == 0) & goes(1, 0)) | ((q1 == 1) & goes(3, 0))
        kinds = [
            ((q2 == 0) & ahead, lambda: copy(along(prim_y, sign))),
            ((q2 == 0) & (q1 == 0) & goes(2, 0), lambda: copy(along(prim_y, -sign))),
            (
                ((q2 == 0) & goes(q1, 1)) | ((q2 == 1) & goes(q1, 3)),
                lambda: copy(along(~prim_y, sign)),
            ),
            ((q2 == 0) & goes(q1, 2), lambda: copy(along(~prim_y, -sign))),
            (shared(q1, q2) & fed, lambda: copy(beside)),
            (q1 + q2 > 0, lambda: copy((a, b + sign))),
        ]
        return k, kinds

    zero = jnp.int32(0)

    def start_own(cls, kinds):
        _, found = links(jnp.int32(cls), zero, zero, True)
        for kind in kinds:
            @pl.when(found[kind][0])
            def _():
                found[kind][1]().start()

    def over_x(cls, step):
        q1, q2 = node(step)
        y0, z0, _ = source(cls, core, q1, q2)
        return shared(q1, q2) & jnp.logical_not(half(cls, y0, z0))

    def forward(cls, step):
        k, found = links(cls, *node(step), False)
        pltpu.make_async_copy(ops_ref.at[k], ops_ref.at[k], op_recv.at[k]).wait()
        for condition, copy in found:
            @pl.when(condition)
            def _():
                copy().start()

    start_own(0, (0, 1))
    start_own(1, (0, 1))

    own = jnp.concatenate(
        [multipole_ref[...].astype(jnp.float32), jnp.zeros((LANES - COEF, BOX), jnp.float32)], axis=0
    ).T
    set_picked(even_ref, own)
    table_ref[0:4, :] = jnp.zeros((4, 128), jnp.float32)
    spread_rows(even_ref, table_ref, 1)
    coarse_out[...] = pad_lanes(coarse_ref[...].astype(jnp.float32))

    has_coarse = b == a // 2

    def coarse_copy(step):
        return pltpu.make_async_remote_copy(
            src_ref=coarse_out.at[pl.ds(pl.multiple_of(a % 2 * 8, 8), 8)], dst_ref=coarse_in,
            send_sem=coarse_send.at[step - 1], recv_sem=coarse_recv,
            device_id=(a, (b + step) % 8), device_id_type=MESH,
        )

    @pl.when(has_coarse)
    def _():
        for step in range(1, 8):
            coarse_copy(step).start()
        coarse_in[...] = coarse_out[pl.ds(pl.multiple_of(a % 2 * 8, 8), 8), :]

    def ghost_copy(n):
        da, db = DIR_SLAB[n], DIR_SUB[n]
        return pltpu.make_async_remote_copy(
            src_ref=ghost_out.at[n], dst_ref=ghost_in.at[n], send_sem=ghost_send.at[n],
            recv_sem=ghost_recv.at[n], device_id=(a + da, b + db), device_id_type=MESH,
        )

    for copy in local[2:]:
        copy.wait()
    for part in range(2):
        pick_rows(ghost_places[part], table_ref, odd_ref)
        ghost_out[4 * part : 4 * part + 4] = picked_value(odd_ref).reshape(4, CAP, LANES)
        for n in range(4 * part, 4 * part + 4):
            @pl.when(exists(DIR_SLAB[n], DIR_SUB[n]))
            def _():
                ghost_copy(n).start()

    start_own(0, (2, 3))
    start_own(1, (2, 3))

    @pl.when(jnp.logical_not(has_coarse))
    def _():
        coarse_copy(1).wait_recv()
    local[0].wait()

    parent = jnp.broadcast_to(coarse_in[pl.ds(b, 1), :], (8, LANES))[:, :COEF].astype(jnp.bfloat16)
    for o in range(8):
        child = lax.dot_general(parent, l2l_ref[o], NT, preferred_element_type=jnp.float32)
        level_one[o : o + 1, :] = pad_lanes(child)[:1]
    parents = level_one[...][:, :COEF].astype(jnp.bfloat16)
    for o in range(8):
        children = pad_lanes(lax.dot_general(parents, l2l_ref[o], NT, preferred_element_type=jnp.float32))
        for c in range(4):
            level_two[c, pl.ds(o, 8, stride=8), :] = children[:, c * 128 : (c + 1) * 128]

    def apply(weight, picked_ref, first=0, count=BOX):
        acc_ref[:, first : first + count] += lax.dot_general(
            weight, picked_value(picked_ref, first, count)[:, :COEF], NT,
            preferred_element_type=jnp.float32,
        )

    acc_ref[...] = jnp.zeros_like(acc_ref)
    even_ref[...] = jnp.zeros_like(even_ref)

    def octant(o, carry):
        early = (o - 8) // 2 + AHEAD

        @pl.when((early > 0) & jnp.logical_not(over_x(o % 2, early)))
        def _():
            forward(o % 2, early)

        for c in range(4):
            rounded = level_two[c].astype(jnp.bfloat16).astype(jnp.float32)
            even_ref[pl.ds(ROW * o + TILE * c, BOX // 8, stride=8 * ROW), :] = rounded
        apply(l2l_ref[o], even_ref)
        for c in range(4):
            even_ref[pl.ds(ROW * o + TILE * c, BOX // 8, stride=8 * ROW), :] = jnp.zeros((BOX // 8, 128), jnp.float32)
        return carry

    lax.fori_loop(0, 8, octant, 0)

    for part in range(2):
        for n in range(4 * part, 4 * part + 4):
            @pl.when(exists(-DIR_SLAB[n], -DIR_SUB[n]))
            def _():
                ghost_copy(n).wait_recv()
        set_picked(odd_ref, ghost_in[4 * part : 4 * part + 4].reshape(BOX, LANES).astype(jnp.float32))
        spread_rows(odd_ref, table_ref, 1 + BOX + part * BOX)

    local[1].wait()

    def ops_of(step):
        return [
            source(jnp.int32(cls), carrier, *node(step))[2]
            for carrier in (core, 1 - core) for cls in (0, 1)
        ]

    def place_copy(k, n):
        return pltpu.make_async_copy(source_place.at[k], place_refs[n], place_sem.at[n])

    def both(n_pick, pick_ref, k_apply, apply_ref):
        for first in range(0, BOX, HALF):
            pick_rows(place_refs[n_pick], table_ref, pick_ref, first, HALF)
            apply(ops_ref[k_apply], apply_ref, first, HALF)

    first_ops = ops_of(jnp.int32(0))
    for n in range(4):
        place_copy(first_ops[n], n).start()
    place_copy(first_ops[0], 0).wait()
    pick_rows(place_refs[0], table_ref, even_ref)
    place_copy(ops_of(jnp.int32(1))[0], 0).start()

    def main(step, carry):
        early, late = step + AHEAD, step + LATE

        def hand_on(cls):
            @pl.when((early < 16) & jnp.logical_not(over_x(cls, early)))
            def _():
                forward(cls, early)

            @pl.when((late < 16) & over_x(cls, late))
            def _():
                forward(cls, late)

        now, then = ops_of(step), ops_of(step + 1)
        after = ops_of(step + 2)
        hand_on(jnp.int32(0))
        place_copy(now[1], 1).wait()
        both(1, odd_ref, now[0], even_ref)

        @pl.when(step < 15)
        def _():
            place_copy(then[1], 1).start()

        hand_on(jnp.int32(1))
        place_copy(now[2], 2).wait()
        both(2, even_ref, now[1], odd_ref)

        @pl.when(step < 15)
        def _():
            place_copy(then[2], 2).start()

        @pl.when(step > 0)
        def _():
            for k in now[2:]:
                pltpu.make_async_copy(ops_ref.at[k], ops_ref.at[k], op_recv.at[k]).wait()

        place_copy(now[3], 3).wait()
        both(3, odd_ref, now[2], even_ref)

        @pl.when(step < 15)
        def _():
            place_copy(then[3], 3).start()
            place_copy(then[0], 0).wait()

        both(0, even_ref, now[3], odd_ref)

        @pl.when(step < 14)
        def _():
            place_copy(after[0], 0).start()

        return carry

    lax.fori_loop(0, 16, main, 0)
    out_ref[...] = acc_ref[...].astype(out_ref.dtype)

    sent = ops_ref.at[pl.ds(0, SENT)]
    pltpu.make_async_copy(sent, sent, op_send).wait()
    for n in range(8):
        @pl.when(exists(DIR_SLAB[n], DIR_SUB[n]))
        def _():
            ghost_copy(n).wait_send()

    @pl.when(has_coarse)
    def _():
        for step in range(1, 8):
            coarse_copy(step).wait_send()


def shards(multipole, send_list, source_slot, m2l_ops, l2l_ops, coarse_exp):
    vmem = pl.BlockSpec(memory_space=pltpu.VMEM)
    hbm = pl.BlockSpec(memory_space=pltpu.HBM)
    f32, bf16 = jnp.float32, jnp.bfloat16
    return pl.pallas_call(
        kernel,
        out_shape=jax.ShapeDtypeStruct((COEF, BOX), bf16),
        in_specs=[vmem, vmem, vmem, hbm, hbm, vmem],
        out_specs=vmem,
        scratch_shapes=[
            pltpu.VMEM((OFFSETS, BOX), jnp.int32),
            pltpu.VMEM((8, CAP), jnp.int32),
            [pltpu.SMEM((BOX,), jnp.int32)] * 4,
            [pltpu.SMEM((BOX,), jnp.int32)] * 2,
            pltpu.VMEM((OFFSETS, COEF, COEF), bf16),
            pltpu.VMEM((8, COEF, COEF), bf16),
            pltpu.VMEM((4 * COLS + 32, 128), f32),
            pltpu.VMEM((BOX * ROW + 16, 128), f32),
            pltpu.VMEM((BOX * ROW + 16, 128), f32),
            pltpu.VMEM((COEF, BOX), f32),
            pltpu.VMEM((8, CAP, LANES), bf16),
            pltpu.VMEM((8, CAP, LANES), bf16),
            pltpu.VMEM((16, LANES), f32),
            pltpu.VMEM((8, LANES), f32),
            pltpu.VMEM((8, LANES), f32),
            pltpu.VMEM((4, 64, 128), f32),
            pltpu.SemaphoreType.DMA((2,)),
            pltpu.SemaphoreType.DMA((4,)),
            pltpu.SemaphoreType.DMA((8,)),
            pltpu.SemaphoreType.DMA,
            pltpu.SemaphoreType.DMA((OFFSETS,)),
            pltpu.SemaphoreType.DMA((8,)),
            pltpu.SemaphoreType.DMA((8,)),
            pltpu.SemaphoreType.DMA((7,)),
            pltpu.SemaphoreType.DMA,
        ],
        compiler_params=pltpu.CompilerParams(
            collective_id=0, has_side_effects=True, vmem_limit_bytes=60 * 2**20
        ),
        name="translate",
    )(multipole, send_list, source_slot, m2l_ops, l2l_ops, coarse_exp.T)


def solution(mesh):
    placed = (
        P(None, ("slab", "sub")),
        P(("slab", "sub"), None, None),
        P(None, ("slab", "sub")),
        P("slab", None, None),
        P(),
        P(None, "sub"),
    )
    return jax.shard_map(
        shards, mesh=mesh, in_specs=placed, out_specs=P(None, ("slab", "sub")), check_vma=False
    )
```

```python
import jax
import jax.numpy as jnp
from jax import lax
from jax.experimental import pallas as pl
from jax.experimental.pallas import tpu as pltpu
from jax.sharding import PartitionSpec as P

DIR_SLAB = (-1, -1, -1, 0, 0, 1, 1, 1)
DIR_SUB = (-1, 0, 1, -1, 1, -1, 0, 1)
COEF, BOX, OFFSETS, CAP, COLS = 456, 512, 64, 128, 1536
LANES = 512
NT = (((1,), (1,)), ((), ()))
MESH = pl.DeviceIdType.MESH
HALF = 256
ROW, TILE = 5, 3
AHEAD = 4
SENT = 60
LATE = 1
ORDER = (
    (0, 0), (1, 0), (2, 0), (0, 2), (0, 1), (3, 0), (1, 1), (2, 2),
    (1, 2), (2, 1), (0, 3), (3, 1), (1, 3), (2, 3), (3, 2), (3, 3),
)
SHARED = {(0, 1), (0, 2), (0, 3), (1, 0), (1, 2), (1, 3), (2, 0), (2, 2), (3, 0), (3, 2)}


def packed(digits, width):
    total = sum(d << (width * i) for i, d in enumerate(digits))
    return total - (1 << 32) if total >= 1 << 31 else total


FIRST = packed([q[0] for q in ORDER], 2)
SECOND = packed([q[1] for q in ORDER], 2)


def children(q):
    q1, q2 = q
    return (
        {(0, 0): (1, 0), (1, 0): (3, 0)}.get(q),
        (2, 0) if q == (0, 0) else None,
        {0: (q1, 1), 1: (q1, 3)}.get(q2),
        (q1, 2) if q2 == 0 else None,
    )


def masks(kind):
    found = [children(q)[kind] for q in ORDER]
    return (
        packed([n is not None and n not in SHARED for n in found], 1),
        packed([n is not None for n in found], 1),
    )


KINDS = tuple(masks(kind) for kind in range(4))
SHARES = packed([q in SHARED for q in ORDER], 1)
TURNS = packed([(q[0] in (1, 2)) ^ (q[1] in (1, 2)) for q in ORDER], 1)


def digit(code, place, width):
    return lax.shift_right_logical(jnp.int32(code), width * place) & (2**width - 1)


def node(step):
    step = jnp.clip(step, 0, 15)
    return digit(FIRST, step, 2), digit(SECOND, step, 2)


def pick_rows(place_ref, table_ref, picked_ref, first=0, count=BOX):
    def chunk(i, carry):
        for u in range(64):
            row = table_ref[pl.ds(place_ref[i * 64 + u], 4), :]
            picked_ref[pl.ds(i * (64 * ROW) + u * ROW, 4, stride=TILE), :] = row
        return carry
    lax.fori_loop(first // 64, (first + count) // 64, chunk, 0, unroll=True)


def spread_rows(picked_ref, table_ref, first):
    def chunk(i, carry):
        for u in range(64):
            place = pl.ds(i * (64 * ROW) + u * ROW, 4, stride=TILE)
            table_ref[pl.ds(first * 4 + i * 256 + u * 4, 4), :] = picked_ref[place, :]
        return carry
    lax.fori_loop(0, BOX // 64, chunk, 0)


def picked_value(picked_ref, first=0, count=BOX):
    tiles = [picked_ref[pl.ds(ROW * first + TILE * c, count, stride=ROW), :] for c in range(4)]
    return jnp.concatenate(tiles, axis=1).astype(jnp.bfloat16)


def set_picked(picked_ref, rows):
    for c in range(4):
        picked_ref[pl.ds(TILE * c, BOX, stride=ROW), :] = rows[:, c * 128 : (c + 1) * 128]


def pad_lanes(rows):
    return jnp.concatenate([rows, jnp.zeros((rows.shape[0], LANES - COEF), rows.dtype)], axis=1)


def kernel(
    multipole_ref, send_list_ref, source_ref, ops_hbm, l2l_hbm, coarse_ref, out_ref,
    source_place, send_place, place_refs, ghost_places, ops_ref, l2l_ref, table_ref, even_ref, odd_ref, acc_ref, ghost_out, ghost_in,
    coarse_out, coarse_in, level_one, level_two,
    local_sem, place_sem, ghost_place_sem, op_send, op_recv, ghost_send, ghost_recv, coarse_send, coarse_recv,
):
    a, b = lax.axis_index("slab"), lax.axis_index("sub")
    z, y, x, core = a >> 2, a & 3, b >> 1, b & 1

    def exists(da, db):
        row, col = a + da, b + db
        return (row >= 0) & (row < 16) & (col >= 0) & (col < 8)

    ghost_in[...] = jnp.zeros_like(ghost_in)
    barrier = pltpu.get_barrier_semaphore()
    for step in range(1, 8):
        pl.semaphore_signal(barrier, inc=1, device_id=(a, (b + step) % 8), device_id_type=MESH)
    for dy, dz in ((1, 0), (3, 0), (0, 1), (0, 3)):
        there = ((z + dz) % 4) * 4 + (y + dy) % 4
        pl.semaphore_signal(barrier, inc=1, device_id=(there, b), device_id_type=MESH)
    greeted = 11
    for da, db in zip(DIR_SLAB, DIR_SUB):
        if da != 0:
            here = exists(da, db)

            @pl.when(here)
            def _():
                pl.semaphore_signal(barrier, inc=1, device_id=(a + da, b + db), device_id_type=MESH)

            greeted = greeted + here.astype(jnp.int32)

    source_place[...] = (source_ref[...] + 1) * 4
    send_place[...] = (jnp.maximum(send_list_ref[0], 0) + 1) * 4
    local = [
        pltpu.make_async_copy(l2l_hbm, l2l_ref, local_sem.at[0]),
        pltpu.make_async_copy(ops_hbm, ops_ref.at[pl.ds(4 * a, 4)], local_sem.at[1]),
    ] + [
        pltpu.make_async_copy(
            send_place.at[n], ghost_places[n // 4].at[pl.ds(n % 4 * CAP, CAP)], ghost_place_sem.at[n]
        )
        for n in range(8)
    ]
    for copy in local:
        copy.start()

    pl.semaphore_wait(barrier, greeted)

    def source(cls, carrier, q1, q2):
        sign = 1 - 2 * carrier
        first = (q1 ^ (q1 >> 1)) * sign
        second = (q2 ^ (q2 >> 1)) * sign
        y0 = (y - jnp.where(cls == 0, first, second)) & 3
        z0 = (z - jnp.where(cls == 0, second, first)) & 3
        return y0, z0, 16 * z0 + 4 * y0 + 2 * carrier + cls

    sign = 1 - 2 * core

    def feeds(cls, step):
        return (x + y + z + cls + digit(TURNS, step, 1)) & 1 == 0

    def links(cls, step, own_op):
        _, _, k = source(cls, core, *node(step))
        fed = feeds(cls, step)
        src = ops_hbm.at[2 * core + cls] if own_op else ops_ref.at[k]

        def goes(kind):
            always, feeding = KINDS[kind]
            return jnp.where(fed, digit(feeding, step, 1), digit(always, step, 1)) == 1

        def copy(device):
            return pltpu.make_async_remote_copy(
                src_ref=src, dst_ref=ops_ref.at[k], send_sem=op_send,
                recv_sem=op_recv.at[k], device_id=device, device_id_type=MESH,
            )

        def along(axis_is_y, by):
            ny = jnp.where(axis_is_y, (y + by) & 3, y)
            nz = jnp.where(axis_is_y, z, (z + by) & 3)
            return (4 * nz + ny, b)

        prim_y = cls == 0
        beside = (a, ((x + sign) & 3) * 2 + core)
        kinds = [
            (goes(0), lambda: copy(along(prim_y, sign))),
            (goes(1), lambda: copy(along(prim_y, -sign))),
            (goes(2), lambda: copy(along(~prim_y, sign))),
            (goes(3), lambda: copy(along(~prim_y, -sign))),
            (fed & (digit(SHARES, step, 1) == 1), lambda: copy(beside)),
            (step > 0, lambda: copy((a, b + sign))),
        ]
        return k, kinds

    zero = jnp.int32(0)

    def start_own(cls, kinds):
        _, found = links(jnp.int32(cls), zero, True)
        for kind in kinds:
            @pl.when(found[kind][0])
            def _():
                found[kind][1]().start()

    def over_x(cls, step):
        step = jnp.clip(step, 0, 15)
        return (digit(SHARES, step, 1) == 1) & jnp.logical_not(feeds(cls, step))

    def forward(cls, step):
        step = jnp.clip(step, 0, 15)
        k, found = links(cls, step, False)
        pltpu.make_async_copy(ops_ref.at[k], ops_ref.at[k], op_recv.at[k]).wait()
        for condition, copy in found:
            @pl.when(condition)
            def _():
                copy().start()

    start_own(0, (0, 1))
    start_own(1, (0, 1))

    own = jnp.concatenate(
        [multipole_ref[...].astype(jnp.float32), jnp.zeros((LANES - COEF, BOX), jnp.float32)], axis=0
    ).T
    set_picked(even_ref, own)
    table_ref[0:4, :] = jnp.zeros((4, 128), jnp.float32)
    spread_rows(even_ref, table_ref, 1)
    coarse_out[...] = pad_lanes(coarse_ref[...].astype(jnp.float32))

    has_coarse = b == a // 2

    def coarse_copy(step):
        return pltpu.make_async_remote_copy(
            src_ref=coarse_out.at[pl.ds(pl.multiple_of(a % 2 * 8, 8), 8)], dst_ref=coarse_in,
            send_sem=coarse_send.at[step - 1], recv_sem=coarse_recv,
            device_id=(a, (b + step) % 8), device_id_type=MESH,
        )

    @pl.when(has_coarse)
    def _():
        for step in range(1, 8):
            coarse_copy(step).start()
        coarse_in[...] = coarse_out[pl.ds(pl.multiple_of(a % 2 * 8, 8), 8), :]

    def ghost_copy(n):
        da, db = DIR_SLAB[n], DIR_SUB[n]
        return pltpu.make_async_remote_copy(
            src_ref=ghost_out.at[n], dst_ref=ghost_in.at[n], send_sem=ghost_send.at[n],
            recv_sem=ghost_recv.at[n], device_id=(a + da, b + db), device_id_type=MESH,
        )

    for copy in local[2:]:
        copy.wait()
    for part in range(2):
        pick_rows(ghost_places[part], table_ref, odd_ref)
        ghost_out[4 * part : 4 * part + 4] = picked_value(odd_ref).reshape(4, CAP, LANES)
        for n in range(4 * part, 4 * part + 4):
            @pl.when(exists(DIR_SLAB[n], DIR_SUB[n]))
            def _():
                ghost_copy(n).start()

    start_own(0, (2, 3))
    start_own(1, (2, 3))

    @pl.when(jnp.logical_not(has_coarse))
    def _():
        coarse_copy(1).wait_recv()
    local[0].wait()

    parent = jnp.broadcast_to(coarse_in[pl.ds(b, 1), :], (8, LANES))[:, :COEF].astype(jnp.bfloat16)
    for o in range(8):
        child = lax.dot_general(parent, l2l_ref[o], NT, preferred_element_type=jnp.float32)
        level_one[o : o + 1, :] = pad_lanes(child)[:1]
    parents = level_one[...][:, :COEF].astype(jnp.bfloat16)
    for o in range(8):
        children = pad_lanes(lax.dot_general(parents, l2l_ref[o], NT, preferred_element_type=jnp.float32))
        for c in range(4):
            level_two[c, pl.ds(o, 8, stride=8), :] = children[:, c * 128 : (c + 1) * 128]

    def apply(weight, picked_ref, first=0, count=BOX):
        acc_ref[:, first : first + count] += lax.dot_general(
            weight, picked_value(picked_ref, first, count)[:, :COEF], NT,
            preferred_element_type=jnp.float32,
        )

    acc_ref[...] = jnp.zeros_like(acc_ref)
    even_ref[...] = jnp.zeros_like(even_ref)

    def octant(o, carry):
        early = (o - 8) // 2 + AHEAD

        @pl.when((early > 0) & jnp.logical_not(over_x(o % 2, early)))
        def _():
            forward(o % 2, early)

        for c in range(4):
            rounded = level_two[c].astype(jnp.bfloat16).astype(jnp.float32)
            even_ref[pl.ds(ROW * o + TILE * c, BOX // 8, stride=8 * ROW), :] = rounded
        apply(l2l_ref[o], even_ref)
        for c in range(4):
            even_ref[pl.ds(ROW * o + TILE * c, BOX // 8, stride=8 * ROW), :] = jnp.zeros((BOX // 8, 128), jnp.float32)
        return carry

    lax.fori_loop(0, 8, octant, 0)

    for part in range(2):
        for n in range(4 * part, 4 * part + 4):
            @pl.when(exists(-DIR_SLAB[n], -DIR_SUB[n]))
            def _():
                ghost_copy(n).wait_recv()
        set_picked(odd_ref, ghost_in[4 * part : 4 * part + 4].reshape(BOX, LANES).astype(jnp.float32))
        spread_rows(odd_ref, table_ref, 1 + BOX + part * BOX)

    local[1].wait()

    def ops_of(step):
        return [
            source(jnp.int32(cls), carrier, *node(step))[2]
            for carrier in (core, 1 - core) for cls in (0, 1)
        ]

    def place_copy(k, n):
        return pltpu.make_async_copy(source_place.at[k], place_refs[n], place_sem.at[n])

    def both(n_pick, pick_ref, k_apply, apply_ref):
        for first in range(0, BOX, HALF):
            pick_rows(place_refs[n_pick], table_ref, pick_ref, first, HALF)
            apply(ops_ref[k_apply], apply_ref, first, HALF)

    first_ops = ops_of(jnp.int32(0))
    for n in range(4):
        place_copy(first_ops[n], n).start()
    place_copy(first_ops[0], 0).wait()
    pick_rows(place_refs[0], table_ref, even_ref)
    place_copy(ops_of(jnp.int32(1))[0], 0).start()

    def main(step, carry):
        early, late = step + AHEAD, step + LATE

        def hand_on(cls):
            @pl.when((early < 16) & jnp.logical_not(over_x(cls, early)))
            def _():
                forward(cls, early)

            @pl.when((late < 16) & over_x(cls, late))
            def _():
                forward(cls, late)

        now, then = ops_of(step), ops_of(step + 1)
        after = ops_of(step + 2)
        hand_on(jnp.int32(0))
        place_copy(now[1], 1).wait()
        both(1, odd_ref, now[0], even_ref)

        @pl.when(step < 15)
        def _():
            place_copy(then[1], 1).start()

        hand_on(jnp.int32(1))
        place_copy(now[2], 2).wait()
        both(2, even_ref, now[1], odd_ref)

        @pl.when(step < 15)
        def _():
            place_copy(then[2], 2).start()

        @pl.when(step > 0)
        def _():
            for k in now[2:]:
                pltpu.make_async_copy(ops_ref.at[k], ops_ref.at[k], op_recv.at[k]).wait()

        place_copy(now[3], 3).wait()
        both(3, odd_ref, now[2], even_ref)

        @pl.when(step < 15)
        def _():
            place_copy(then[3], 3).start()
            place_copy(then[0], 0).wait()

        both(0, even_ref, now[3], odd_ref)

        @pl.when(step < 14)
        def _():
            place_copy(after[0], 0).start()

        return carry

    lax.fori_loop(0, 16, main, 0)
    out_ref[...] = acc_ref[...].astype(out_ref.dtype)

    sent = ops_ref.at[pl.ds(0, SENT)]
    pltpu.make_async_copy(sent, sent, op_send).wait()
    for n in range(8):
        @pl.when(exists(DIR_SLAB[n], DIR_SUB[n]))
        def _():
            ghost_copy(n).wait_send()

    @pl.when(has_coarse)
    def _():
        for step in range(1, 8):
            coarse_copy(step).wait_send()


def shards(multipole, send_list, source_slot, m2l_ops, l2l_ops, coarse_exp):
    vmem = pl.BlockSpec(memory_space=pltpu.VMEM)
    hbm = pl.BlockSpec(memory_space=pltpu.HBM)
    f32, bf16 = jnp.float32, jnp.bfloat16
    return pl.pallas_call(
        kernel,
        out_shape=jax.ShapeDtypeStruct((COEF, BOX), bf16),
        in_specs=[vmem, vmem, vmem, hbm, hbm, vmem],
        out_specs=vmem,
        scratch_shapes=[
            pltpu.VMEM((OFFSETS, BOX), jnp.int32),
            pltpu.VMEM((8, CAP), jnp.int32),
            [pltpu.SMEM((BOX,), jnp.int32)] * 4,
            [pltpu.SMEM((BOX,), jnp.int32)] * 2,
            pltpu.VMEM((OFFSETS, COEF, COEF), bf16),
            pltpu.VMEM((8, COEF, COEF), bf16),
            pltpu.VMEM((4 * COLS + 32, 128), f32),
            pltpu.VMEM((BOX * ROW + 16, 128), f32),
            pltpu.VMEM((BOX * ROW + 16, 128), f32),
            pltpu.VMEM((COEF, BOX), f32),
            pltpu.VMEM((8, CAP, LANES), bf16),
            pltpu.VMEM((8, CAP, LANES), bf16),
            pltpu.VMEM((16, LANES), f32),
            pltpu.VMEM((8, LANES), f32),
            pltpu.VMEM((8, LANES), f32),
            pltpu.VMEM((4, 64, 128), f32),
            pltpu.SemaphoreType.DMA((2,)),
            pltpu.SemaphoreType.DMA((4,)),
            pltpu.SemaphoreType.DMA((8,)),
            pltpu.SemaphoreType.DMA,
            pltpu.SemaphoreType.DMA((OFFSETS,)),
            pltpu.SemaphoreType.DMA((8,)),
            pltpu.SemaphoreType.DMA((8,)),
            pltpu.SemaphoreType.DMA((7,)),
            pltpu.SemaphoreType.DMA,
        ],
        compiler_params=pltpu.CompilerParams(
            collective_id=0, has_side_effects=True, vmem_limit_bytes=60 * 2**20
        ),
        name="translate",
    )(multipole, send_list, source_slot, m2l_ops, l2l_ops, coarse_exp.T)


def solution(mesh):
    placed = (
        P(None, ("slab", "sub")),
        P(("slab", "sub"), None, None),
        P(None, ("slab", "sub")),
        P("slab", None, None),
        P(),
        P(None, "sub"),
    )
    return jax.shard_map(
        shards, mesh=mesh, in_specs=placed, out_specs=P(None, ("slab", "sub")), check_vma=False
    )
```

```python
import jax
import jax.numpy as jnp
from jax import lax
from jax.experimental import pallas as pl
from jax.experimental.pallas import tpu as pltpu
from jax.sharding import PartitionSpec as P

DIR_SLAB = (-1, -1, -1, 0, 0, 1, 1, 1)
DIR_SUB = (-1, 0, 1, -1, 1, -1, 0, 1)
COEF, BOX, OFFSETS, CAP, COLS = 456, 512, 64, 128, 1536
LANES = 512
NT = (((1,), (1,)), ((), ()))
MESH = pl.DeviceIdType.MESH
HALF = 256
ROW, TILE = 5, 3
AHEAD = 3
SENT = 60
LATE = 1
ORDER = (
    (0, 0), (1, 0), (2, 0), (0, 2), (0, 1), (3, 0), (1, 1), (2, 2),
    (1, 2), (2, 1), (0, 3), (3, 1), (1, 3), (2, 3), (3, 2), (3, 3),
)
SHARED = {(0, 1), (0, 2), (0, 3), (1, 0), (1, 2), (1, 3), (2, 0), (2, 2), (3, 0), (3, 2)}


def packed(digits, width):
    total = sum(d << (width * i) for i, d in enumerate(digits))
    return total - (1 << 32) if total >= 1 << 31 else total


FIRST = packed([q[0] for q in ORDER], 2)
SECOND = packed([q[1] for q in ORDER], 2)


def children(q):
    q1, q2 = q
    return (
        {(0, 0): (1, 0), (1, 0): (3, 0)}.get(q),
        (2, 0) if q == (0, 0) else None,
        {0: (q1, 1), 1: (q1, 3)}.get(q2),
        (q1, 2) if q2 == 0 else None,
    )


def masks(kind):
    found = [children(q)[kind] for q in ORDER]
    return (
        packed([n is not None and n not in SHARED for n in found], 1),
        packed([n is not None for n in found], 1),
    )


KINDS = tuple(masks(kind) for kind in range(4))
SHARES = packed([q in SHARED for q in ORDER], 1)
TURNS = packed([(q[0] in (1, 2)) ^ (q[1] in (1, 2)) for q in ORDER], 1)


def digit(code, place, width):
    return lax.shift_right_logical(jnp.int32(code), width * place) & (2**width - 1)


def node(step):
    step = jnp.clip(step, 0, 15)
    return digit(FIRST, step, 2), digit(SECOND, step, 2)


def pick_rows(place_ref, table_ref, picked_ref, first=0, count=BOX):
    def chunk(i, carry):
        for u in range(64):
            row = table_ref[pl.ds(place_ref[i * 64 + u], 4), :]
            picked_ref[pl.ds(i * (64 * ROW) + u * ROW, 4, stride=TILE), :] = row
        return carry
    lax.fori_loop(first // 64, (first + count) // 64, chunk, 0, unroll=True)


def spread_rows(picked_ref, table_ref, first):
    def chunk(i, carry):
        for u in range(64):
            place = pl.ds(i * (64 * ROW) + u * ROW, 4, stride=TILE)
            table_ref[pl.ds(first * 4 + i * 256 + u * 4, 4), :] = picked_ref[place, :]
        return carry
    lax.fori_loop(0, BOX // 64, chunk, 0)


def picked_value(picked_ref, first=0, count=BOX):
    tiles = [picked_ref[pl.ds(ROW * first + TILE * c, count, stride=ROW), :] for c in range(4)]
    return jnp.concatenate(tiles, axis=1).astype(jnp.bfloat16)


def set_picked(picked_ref, rows):
    for c in range(4):
        picked_ref[pl.ds(TILE * c, BOX, stride=ROW), :] = rows[:, c * 128 : (c + 1) * 128]


def pad_lanes(rows):
    return jnp.concatenate([rows, jnp.zeros((rows.shape[0], LANES - COEF), rows.dtype)], axis=1)


def kernel(
    multipole_ref, send_list_ref, source_ref, ops_hbm, l2l_hbm, coarse_ref, out_ref,
    source_place, send_place, place_refs, ghost_places, ops_ref, l2l_ref, table_ref, even_ref, odd_ref, acc_ref, ghost_out, ghost_in,
    coarse_out, coarse_in, level_one, level_two,
    local_sem, place_sem, ghost_place_sem, op_send, op_recv, ghost_send, ghost_recv, coarse_send, coarse_recv,
):
    a, b = lax.axis_index("slab"), lax.axis_index("sub")
    z, y, x, core = a >> 2, a & 3, b >> 1, b & 1

    def exists(da, db):
        row, col = a + da, b + db
        return (row >= 0) & (row < 16) & (col >= 0) & (col < 8)

    ghost_in[...] = jnp.zeros_like(ghost_in)
    barrier = pltpu.get_barrier_semaphore()
    for step in range(1, 8):
        pl.semaphore_signal(barrier, inc=1, device_id=(a, (b + step) % 8), device_id_type=MESH)
    for dy, dz in ((1, 0), (3, 0), (0, 1), (0, 3)):
        there = ((z + dz) % 4) * 4 + (y + dy) % 4
        pl.semaphore_signal(barrier, inc=1, device_id=(there, b), device_id_type=MESH)
    greeted = 11
    for da, db in zip(DIR_SLAB, DIR_SUB):
        if da != 0:
            here = exists(da, db)

            @pl.when(here)
            def _():
                pl.semaphore_signal(barrier, inc=1, device_id=(a + da, b + db), device_id_type=MESH)

            greeted = greeted + here.astype(jnp.int32)

    source_place[...] = (source_ref[...] + 1) * 4
    send_place[...] = (jnp.maximum(send_list_ref[0], 0) + 1) * 4
    local = [
        pltpu.make_async_copy(l2l_hbm, l2l_ref, local_sem.at[0]),
        pltpu.make_async_copy(ops_hbm, ops_ref.at[pl.ds(4 * a, 4)], local_sem.at[1]),
    ] + [
        pltpu.make_async_copy(
            send_place.at[n], ghost_places[n // 4].at[pl.ds(n % 4 * CAP, CAP)], ghost_place_sem.at[n]
        )
        for n in range(8)
    ]
    for copy in local:
        copy.start()

    pl.semaphore_wait(barrier, greeted)

    def source(cls, carrier, q1, q2):
        sign = 1 - 2 * carrier
        first = (q1 ^ (q1 >> 1)) * sign
        second = (q2 ^ (q2 >> 1)) * sign
        y0 = (y - jnp.where(cls == 0, first, second)) & 3
        z0 = (z - jnp.where(cls == 0, second, first)) & 3
        return y0, z0, 16 * z0 + 4 * y0 + 2 * carrier + cls

    sign = 1 - 2 * core

    def feeds(cls, step):
        return (x + y + z + cls + digit(TURNS, step, 1)) & 1 == 0

    def links(cls, step, own_op):
        _, _, k = source(cls, core, *node(step))
        fed = feeds(cls, step)
        src = ops_hbm.at[2 * core + cls] if own_op else ops_ref.at[k]

        def goes(kind):
            always, feeding = KINDS[kind]
            return jnp.where(fed, digit(feeding, step, 1), digit(always, step, 1)) == 1

        def copy(device):
            return pltpu.make_async_remote_copy(
                src_ref=src, dst_ref=ops_ref.at[k], send_sem=op_send,
                recv_sem=op_recv.at[k], device_id=device, device_id_type=MESH,
            )

        def along(axis_is_y, by):
            ny = jnp.where(axis_is_y, (y + by) & 3, y)
            nz = jnp.where(axis_is_y, z, (z + by) & 3)
            return (4 * nz + ny, b)

        prim_y = cls == 0
        beside = (a, ((x + sign) & 3) * 2 + core)
        kinds = [
            (goes(0), lambda: copy(along(prim_y, sign))),
            (goes(1), lambda: copy(along(prim_y, -sign))),
            (goes(2), lambda: copy(along(~prim_y, sign))),
            (goes(3), lambda: copy(along(~prim_y, -sign))),
            (fed & (digit(SHARES, step, 1) == 1), lambda: copy(beside)),
            (step > 0, lambda: copy((a, b + sign))),
        ]
        return k, kinds

    zero = jnp.int32(0)

    def start_own(cls, kinds):
        _, found = links(jnp.int32(cls), zero, True)
        for kind in kinds:
            @pl.when(found[kind][0])
            def _():
                found[kind][1]().start()

    def over_x(cls, step):
        step = jnp.clip(step, 0, 15)
        return (digit(SHARES, step, 1) == 1) & jnp.logical_not(feeds(cls, step))

    def forward(cls, step):
        step = jnp.clip(step, 0, 15)
        k, found = links(cls, step, False)
        pltpu.make_async_copy(ops_ref.at[k], ops_ref.at[k], op_recv.at[k]).wait()
        for condition, copy in found:
            @pl.when(condition)
            def _():
                copy().start()

    start_own(0, (0, 1))
    start_own(1, (0, 1))

    own = jnp.concatenate(
        [multipole_ref[...].astype(jnp.float32), jnp.zeros((LANES - COEF, BOX), jnp.float32)], axis=0
    ).T
    set_picked(even_ref, own)
    table_ref[0:4, :] = jnp.zeros((4, 128), jnp.float32)
    spread_rows(even_ref, table_ref, 1)
    coarse_out[...] = pad_lanes(coarse_ref[...].astype(jnp.float32))

    has_coarse = b == a // 2

    def coarse_copy(step):
        return pltpu.make_async_remote_copy(
            src_ref=coarse_out.at[pl.ds(pl.multiple_of(a % 2 * 8, 8), 8)], dst_ref=coarse_in,
            send_sem=coarse_send.at[step - 1], recv_sem=coarse_recv,
            device_id=(a, (b + step) % 8), device_id_type=MESH,
        )

    @pl.when(has_coarse)
    def _():
        for step in range(1, 8):
            coarse_copy(step).start()
        coarse_in[...] = coarse_out[pl.ds(pl.multiple_of(a % 2 * 8, 8), 8), :]

    def ghost_copy(n):
        da, db = DIR_SLAB[n], DIR_SUB[n]
        return pltpu.make_async_remote_copy(
            src_ref=ghost_out.at[n], dst_ref=ghost_in.at[n], send_sem=ghost_send.at[n],
            recv_sem=ghost_recv.at[n], device_id=(a + da, b + db), device_id_type=MESH,
        )

    for copy in local[2:]:
        copy.wait()
    for part in range(2):
        pick_rows(ghost_places[part], table_ref, odd_ref)
        ghost_out[4 * part : 4 * part + 4] = picked_value(odd_ref).reshape(4, CAP, LANES)
        for n in range(4 * part, 4 * part + 4):
            @pl.when(exists(DIR_SLAB[n], DIR_SUB[n]))
            def _():
                ghost_copy(n).start()

    start_own(0, (2, 3))
    start_own(1, (2, 3))

    @pl.when(jnp.logical_not(has_coarse))
    def _():
        coarse_copy(1).wait_recv()
    local[0].wait()

    parent = jnp.broadcast_to(coarse_in[pl.ds(b, 1), :], (8, LANES))[:, :COEF].astype(jnp.bfloat16)
    for o in range(8):
        child = lax.dot_general(parent, l2l_ref[o], NT, preferred_element_type=jnp.float32)
        level_one[o : o + 1, :] = pad_lanes(child)[:1]
    parents = level_one[...][:, :COEF].astype(jnp.bfloat16)
    for o in range(8):
        children = pad_lanes(lax.dot_general(parents, l2l_ref[o], NT, preferred_element_type=jnp.float32))
        for c in range(4):
            level_two[c, pl.ds(o, 8, stride=8), :] = children[:, c * 128 : (c + 1) * 128]

    def apply(weight, picked_ref, first=0, count=BOX):
        acc_ref[:, first : first + count] += lax.dot_general(
            weight, picked_value(picked_ref, first, count)[:, :COEF], NT,
            preferred_element_type=jnp.float32,
        )

    acc_ref[...] = jnp.zeros_like(acc_ref)
    even_ref[...] = jnp.zeros_like(even_ref)

    def octant(o, carry):
        early = (o - 8) // 2 + AHEAD

        @pl.when((early > 0) & jnp.logical_not(over_x(o % 2, early)))
        def _():
            forward(o % 2, early)

        for c in range(4):
            rounded = level_two[c].astype(jnp.bfloat16).astype(jnp.float32)
            even_ref[pl.ds(ROW * o + TILE * c, BOX // 8, stride=8 * ROW), :] = rounded
        apply(l2l_ref[o], even_ref)
        for c in range(4):
            even_ref[pl.ds(ROW * o + TILE * c, BOX // 8, stride=8 * ROW), :] = jnp.zeros((BOX // 8, 128), jnp.float32)
        return carry

    lax.fori_loop(0, 8, octant, 0)

    for part in range(2):
        for n in range(4 * part, 4 * part + 4):
            @pl.when(exists(-DIR_SLAB[n], -DIR_SUB[n]))
            def _():
                ghost_copy(n).wait_recv()
        set_picked(odd_ref, ghost_in[4 * part : 4 * part + 4].reshape(BOX, LANES).astype(jnp.float32))
        spread_rows(odd_ref, table_ref, 1 + BOX + part * BOX)

    local[1].wait()

    def ops_of(step):
        return [
            source(jnp.int32(cls), carrier, *node(step))[2]
            for carrier in (core, 1 - core) for cls in (0, 1)
        ]

    def place_copy(k, n):
        return pltpu.make_async_copy(source_place.at[k], place_refs[n], place_sem.at[n])

    def both(n_pick, pick_ref, k_apply, apply_ref):
        for first in range(0, BOX, HALF):
            pick_rows(place_refs[n_pick], table_ref, pick_ref, first, HALF)
            apply(ops_ref[k_apply], apply_ref, first, HALF)

    first_ops = ops_of(jnp.int32(0))
    for n in range(4):
        place_copy(first_ops[n], n).start()
    place_copy(first_ops[0], 0).wait()
    pick_rows(place_refs[0], table_ref, even_ref)
    place_copy(ops_of(jnp.int32(1))[0], 0).start()

    def main(step, carry):
        early, late = step + AHEAD, step + LATE

        def hand_on(cls):
            @pl.when((early < 16) & jnp.logical_not(over_x(cls, early)))
            def _():
                forward(cls, early)

            @pl.when((late < 16) & over_x(cls, late))
            def _():
                forward(cls, late)

        now, then = ops_of(step), ops_of(step + 1)
        after = ops_of(step + 2)
        hand_on(jnp.int32(0))
        place_copy(now[1], 1).wait()
        both(1, odd_ref, now[0], even_ref)

        @pl.when(step < 15)
        def _():
            place_copy(then[1], 1).start()

        hand_on(jnp.int32(1))
        place_copy(now[2], 2).wait()
        both(2, even_ref, now[1], odd_ref)

        @pl.when(step < 15)
        def _():
            place_copy(then[2], 2).start()

        @pl.when(step > 0)
        def _():
            for k in now[2:]:
                pltpu.make_async_copy(ops_ref.at[k], ops_ref.at[k], op_recv.at[k]).wait()

        place_copy(now[3], 3).wait()
        both(3, odd_ref, now[2], even_ref)

        @pl.when(step < 15)
        def _():
            place_copy(then[3], 3).start()
            place_copy(then[0], 0).wait()

        both(0, even_ref, now[3], odd_ref)

        @pl.when(step < 14)
        def _():
            place_copy(after[0], 0).start()

        return carry

    lax.fori_loop(0, 16, main, 0)
    out_ref[...] = acc_ref[...].astype(out_ref.dtype)

    sent = ops_ref.at[pl.ds(0, SENT)]
    pltpu.make_async_copy(sent, sent, op_send).wait()
    for n in range(8):
        @pl.when(exists(DIR_SLAB[n], DIR_SUB[n]))
        def _():
            ghost_copy(n).wait_send()

    @pl.when(has_coarse)
    def _():
        for step in range(1, 8):
            coarse_copy(step).wait_send()


def shards(multipole, send_list, source_slot, m2l_ops, l2l_ops, coarse_exp):
    vmem = pl.BlockSpec(memory_space=pltpu.VMEM)
    hbm = pl.BlockSpec(memory_space=pltpu.HBM)
    f32, bf16 = jnp.float32, jnp.bfloat16
    return pl.pallas_call(
        kernel,
        out_shape=jax.ShapeDtypeStruct((COEF, BOX), bf16),
        in_specs=[vmem, vmem, vmem, hbm, hbm, vmem],
        out_specs=vmem,
        scratch_shapes=[
            pltpu.VMEM((OFFSETS, BOX), jnp.int32),
            pltpu.VMEM((8, CAP), jnp.int32),
            [pltpu.SMEM((BOX,), jnp.int32)] * 4,
            [pltpu.SMEM((BOX,), jnp.int32)] * 2,
            pltpu.VMEM((OFFSETS, COEF, COEF), bf16),
            pltpu.VMEM((8, COEF, COEF), bf16),
            pltpu.VMEM((4 * COLS + 32, 128), f32),
            pltpu.VMEM((BOX * ROW + 16, 128), f32),
            pltpu.VMEM((BOX * ROW + 16, 128), f32),
            pltpu.VMEM((COEF, BOX), f32),
            pltpu.VMEM((8, CAP, LANES), bf16),
            pltpu.VMEM((8, CAP, LANES), bf16),
            pltpu.VMEM((16, LANES), f32),
            pltpu.VMEM((8, LANES), f32),
            pltpu.VMEM((8, LANES), f32),
            pltpu.VMEM((4, 64, 128), f32),
            pltpu.SemaphoreType.DMA((2,)),
            pltpu.SemaphoreType.DMA((4,)),
            pltpu.SemaphoreType.DMA((8,)),
            pltpu.SemaphoreType.DMA,
            pltpu.SemaphoreType.DMA((OFFSETS,)),
            pltpu.SemaphoreType.DMA((8,)),
            pltpu.SemaphoreType.DMA((8,)),
            pltpu.SemaphoreType.DMA((7,)),
            pltpu.SemaphoreType.DMA,
        ],
        compiler_params=pltpu.CompilerParams(
            collective_id=0, has_side_effects=True, vmem_limit_bytes=60 * 2**20
        ),
        name="translate",
    )(multipole, send_list, source_slot, m2l_ops, l2l_ops, coarse_exp.T)


def solution(mesh):
    placed = (
        P(None, ("slab", "sub")),
        P(("slab", "sub"), None, None),
        P(None, ("slab", "sub")),
        P("slab", None, None),
        P(),
        P(None, "sub"),
    )
    return jax.shard_map(
        shards, mesh=mesh, in_specs=placed, out_specs=P(None, ("slab", "sub")), check_vma=False
    )
```
